128 devices in a mesh: expert: 32 (over x, y, core), dp: 4 (over z).
Axes of the slice: x: 4, y: 4, z: 4, core: 2. Of those that a mesh axis runs over, the one named last changes fastest.
Arguments:
- tokens: bfloat16 [16384, 2048], P(('expert', 'dp')), may hold values from -6 to 6
- cotangent: bfloat16 [16384, 2048], P(('expert', 'dp')), may hold values from -6 to 6
- router_probs: float32 [16384, 6], P(('expert', 'dp')), may hold values from 0.1 to 0.6
- routes: int32 [16384, 6], P(('expert', 'dp')), may hold values from 0 to 63, all different within a row; in each aligned block of 128 rows (0 to 127, 128 to 255, ...) at most 15 rows name the same one
- partner: int32 [32], replicated, may hold values from 0 to 31, as said below
- gate_weight: bfloat16 [64, 2048, 768], P('expert'), may hold values from -0.125 to 0.125
- up_weight: bfloat16 [64, 2048, 768], P('expert'), may hold values from -0.125 to 0.125
- down_weight: bfloat16 [64, 768, 2048], P('expert'), may hold values from -0.21875 to 0.21875
Outputs:
- output: bfloat16 [16384, 2048], P(('expert', 'dp'))
- token_grad: bfloat16 [16384, 2048], P(('expert', 'dp'))
- expert_grads: bfloat16 [768, 64, 3, 2048], P('dp', 'expert')
The draws below stay inside these ranges and needn't reach their ends.
Inputs may be any that keep to these rules, and one draw needn't show every extreme that they name: `routes`: each token names 6 different experts. Within the 128 rows of one device no expert is named by more than 15 rows, a bound that some block reaches of them. partner[j] is j or (j + 16) mod 32, and partner[partner[j]] = j.
All inputs are finite; a program needn't handle non-finite values.
Results may differ from the reference program's by a relative error of at most 0.0095.
Values may be sent and summed in bfloat16 or wider, within the bound.
No kernel may reach another device: no remote copies, remote signals or barrier semaphores. Data moves between devices by JAX's collectives and lax.ppermute only.
A program may use at most 192 MiB of HBM per device.

```python
import math
import jax
import jax.numpy as jnp
import numpy as np
from jax import lax

D = 2048
FF = 768
TOK_DEV = 128
TOPK = 6
EXP_DEV = 2
EXPERTS = 64
CAP = 15
TOKENS = 16384
N_EXPERT = 32
N_DP = 4


def draw_partner(key, part):
    half_axis = N_EXPERT // 2
    flags = jax.random.randint(key, (half_axis,), 0, 2)
    flags = jnp.concatenate([flags, flags])
    position = jnp.arange(N_EXPERT)
    return jnp.where(flags == 1, (position + half_axis) % N_EXPERT, position).astype(jnp.int32)


def level_of(own_key, dims, pieces, least, high):
    def one(axis_at, shards_of):
        heights = jax.random.uniform(jax.random.fold_in(jax.random.fold_in(own_key, 6), axis_at), (shards_of,), jnp.float32, least / len(pieces), high / len(pieces))
        return jnp.repeat(jnp.exp(heights), dims[axis_at] // shards_of).reshape((-1,) + (1,) * (len(dims) - axis_at - 1))

    loudness = one(*pieces[0])
    for cut in pieces[1:]:
        loudness = loudness * one(*cut)
    return loudness


def shared_out(stream_key, own, number, rows, count, top, limit, skew):
    sequence = jax.random.permutation(stream_key, count)
    crowded, usual = load_shares(count, rows * top, limit, skew, True), load_shares(count, rows * top, limit, skew, False)
    places = jnp.arange(count)

    def named(lengths, offset_by):
        used = int((lengths > 0).sum())
        fixed = max(1, used // 4)
        moved = fixed + (places - fixed + offset_by * (used - fixed)) % max(1, count - fixed)
        return jnp.zeros((count,), jnp.int32).at[sequence[jnp.where(places < fixed, places, moved)]].set(jnp.asarray(lengths, jnp.int32))

    lengths = jnp.where(number % 4 == 0, named(crowded, number // 4), named(usual, number - number // 4 - 1))
    mixed = jax.random.permutation(jax.random.fold_in(own, 3), count)
    donor, sink = mixed[0:count // 2 * 2:2], mixed[1:count // 2 * 2:2]
    slack = jnp.minimum(lengths[donor] - 1, limit - lengths[sink]) // 2
    slack = jnp.where((donor == sequence[0]) | (sink == sequence[0]) | (lengths[sink] == 0), 0, jnp.maximum(slack, 0))
    moved = jax.random.randint(jax.random.fold_in(own, 4), (count // 2,), 0, 1 << 20) % (slack + 1)
    lengths = lengths.at[donor].add(-moved).at[sink].add(moved)
    items = jnp.searchsorted(jnp.cumsum(lengths), jnp.arange(rows * top), side="right").astype(jnp.int32)
    grid = items.reshape(top, rows).T
    grid = grid[jax.random.permutation(jax.random.fold_in(own, 1), rows)]
    offset_by = jax.random.randint(jax.random.fold_in(own, 2), (rows, 1), 0, top)
    return jnp.take_along_axis(grid, (jnp.arange(top)[None, :] + offset_by) % top, axis=1)


def load_shares(number_of, total, bound, skew, full):
    weights = [(1 << 20) // math.isqrt(standing ** skew) + 1 for standing in range(1, number_of + 1)]
    largest = bound if full else min(bound, max(-(-total // number_of), total * weights[0] // sum(weights)))
    least = 1 if total - largest >= number_of - 1 else 0
    given, spare = [largest] + [least] * (number_of - 1), total - largest - least * (number_of - 1)
    while spare > 0:
        free = [i for i in range(1, number_of) if given[i] < largest] or [i for i in range(1, number_of) if given[i] < bound]
        mass, left = sum([weights[i] for i in free]), spare
        for i in free:
            more = min(bound - given[i], max(1, left * weights[i] // mass), spare)
            given[i] = given[i] + more
            spare = spare - more
    return np.array(given)


def gaussian(key, dims, deviation, reach, cuts=(), kind=jnp.bfloat16):
    drawn = jax.random.normal(key, dims, jnp.float32) * deviation
    if len(cuts) > 0:
        drawn = level_of(key, dims, cuts, -0.22, 0.18) * drawn
    return jnp.clip(drawn, min=-reach, max=reach).astype(kind)


def setup_inputs(seed: int = 0) -> dict:
    key_of = jax.random.split(jax.random.key(seed), 9)
    tokens = gaussian(key_of[0], (TOKENS, D), 1.0, 6.0, ((0, 128),))
    cotangent = gaussian(key_of[1], (TOKENS, D), 1.0, 6.0, ((0, 128),))
    router_probs = jnp.clip(0.1 + 0.5 * jax.random.uniform(key_of[2], (TOKENS, TOPK), jnp.float32) ** level_of(key_of[2], (TOKENS, TOPK), ((0, 128),), -0.2, 0.2), 0.1, 0.6)
    routes_keys = jax.random.split(jax.random.fold_in(key_of[3], 1), TOKENS // TOK_DEV)
    routes_turns = jax.random.permutation(jax.random.fold_in(key_of[3], 3), TOKENS // TOK_DEV)
    routes = jax.vmap(lambda own, number: shared_out(jax.random.fold_in(key_of[3], 2), own, number, TOK_DEV, EXPERTS, TOPK, CAP, 2))(routes_keys, routes_turns).reshape((TOKENS, TOPK))
    partner = draw_partner(jax.random.fold_in(key_of[8], 71), 0)
    gate_weight = gaussian(key_of[5], (EXPERTS, D, FF), D ** -0.5, 0.125, ((0, 32),))
    up_weight = gaussian(key_of[6], (EXPERTS, D, FF), D ** -0.5, 0.125, ((0, 32),))
    down_weight = gaussian(key_of[7], (EXPERTS, FF, D), FF ** -0.5, 0.21875, ((0, 32),))
    return dict(tokens=tokens, cotangent=cotangent, router_probs=router_probs, routes=routes, partner=partner, gate_weight=gate_weight, up_weight=up_weight, down_weight=down_weight)


def reference(tokens, cotangent, router_probs, routes, partner, gate_weight, up_weight, down_weight):
    assigned = TOKENS * TOPK
    flat_routes = routes.reshape(-1).astype(jnp.int32)
    token_of = (jnp.arange(assigned, dtype=jnp.int32) // TOPK).astype(jnp.int32)
    group_of = ((token_of // TOK_DEV) % N_DP).astype(jnp.int32)
    sort_key = (flat_routes * N_DP + group_of).astype(jnp.int32)
    sorted_at = jnp.argsort(sort_key, stable=True).astype(jnp.int32)
    bin_count = EXPERTS * N_DP
    counts = jnp.sum((sort_key[None, :] == jnp.arange(bin_count, dtype=jnp.int32)[:, None]).astype(jnp.int32), axis=1)
    starts = (jnp.cumsum(counts) - counts).astype(jnp.int32)
    most_rows = CAP * N_EXPERT
    padded_order = jnp.concatenate([sorted_at, jnp.full((most_rows,), assigned, jnp.int32)])
    zero_row = jnp.zeros((1, D), tokens.dtype)
    padded_tokens = jnp.concatenate([tokens, zero_row], axis=0)
    padded_cot = jnp.concatenate([cotangent, zero_row], axis=0)
    padded_probs = jnp.concatenate([router_probs.reshape(-1), jnp.zeros((1,), jnp.float32)])
    position = jnp.arange(most_rows, dtype=jnp.int32)

    def per_expert(expert):
        slot_id = (partner[expert // EXP_DEV] * EXP_DEV + expert % EXP_DEV).astype(jnp.int32)
        gate_w = gate_weight[slot_id].astype(jnp.float32)
        up_w = up_weight[slot_id].astype(jnp.float32)
        down_w = down_weight[slot_id].astype(jnp.float32)
        out_list = []
        dx_list = []
        index_list = []
        grad_total = jnp.zeros((3, FF, D), jnp.float32)
        for group_id in range(N_DP):
            begin_at = starts[expert * N_DP + group_id]
            live_count = counts[expert * N_DP + group_id]
            row_index = lax.dynamic_slice(padded_order, (begin_at,), (most_rows,))
            row_index = jnp.where(position < live_count, row_index, assigned).astype(jnp.int32)
            row_token = (row_index // TOPK).astype(jnp.int32)
            expert_in = padded_tokens[row_token].astype(jnp.float32)
            scaled = (padded_probs[row_index][:, None] * padded_cot[row_token].astype(jnp.float32)).astype(jnp.bfloat16)
            expert_cot = lax.optimization_barrier(scaled).astype(jnp.float32)
            gate_pre = jnp.dot(expert_in, gate_w, preferred_element_type=jnp.float32)
            up_proj = jnp.dot(expert_in, up_w, preferred_element_type=jnp.float32)
            sigmoid_gate = jax.nn.sigmoid(gate_pre)
            activated = gate_pre * sigmoid_gate
            hidden = lax.optimization_barrier((activated * up_proj).astype(jnp.bfloat16)).astype(jnp.float32)
            out_rows = jnp.dot(hidden, down_w, preferred_element_type=jnp.float32).astype(jnp.bfloat16)
            grad_hidden = jnp.dot(expert_cot, down_w.T, preferred_element_type=jnp.float32)
            grad_gate = (grad_hidden * up_proj * sigmoid_gate * (1.0 + gate_pre * (1.0 - sigmoid_gate))).astype(jnp.bfloat16)
            grad_up = (grad_hidden * activated).astype(jnp.bfloat16)
            grad_gate = lax.optimization_barrier(grad_gate).astype(jnp.float32)
            grad_up = lax.optimization_barrier(grad_up).astype(jnp.float32)
            dx_rows = (jnp.dot(grad_gate, gate_w.T, preferred_element_type=jnp.float32)
                       + jnp.dot(grad_up, up_w.T, preferred_element_type=jnp.float32)).astype(jnp.bfloat16)
            partial_value = jnp.stack([
                jnp.dot(grad_gate.T, expert_in, preferred_element_type=jnp.float32),
                jnp.dot(grad_up.T, expert_in, preferred_element_type=jnp.float32),
                jnp.dot(hidden.T, expert_cot, preferred_element_type=jnp.float32)], axis=0)
            partial_value = lax.optimization_barrier(partial_value.astype(jnp.bfloat16))
            grad_total = grad_total + partial_value.astype(jnp.float32)
            out_list.append(out_rows)
            dx_list.append(dx_rows)
            index_list.append(row_index)
        return (jnp.stack(out_list), jnp.stack(dx_list), jnp.stack(index_list), grad_total.astype(jnp.bfloat16))

    out_rows, dx_rows, indices, grads = lax.map(per_expert, jnp.arange(EXPERTS, dtype=jnp.int32))
    flat_index = indices.reshape(-1)
    assign_out = jnp.zeros((assigned + 1, D), jnp.bfloat16).at[flat_index].set(out_rows.reshape(-1, D).astype(jnp.bfloat16))
    assign_dx = jnp.zeros((assigned + 1, D), jnp.bfloat16).at[flat_index].set(dx_rows.reshape(-1, D).astype(jnp.bfloat16))
    picked_out = assign_out[:assigned].reshape(TOKENS, TOPK, D).astype(jnp.float32)
    picked_dx = assign_dx[:assigned].reshape(TOKENS, TOPK, D).astype(jnp.float32)
    output = jnp.sum(router_probs[:, :, None] * picked_out, axis=1).astype(jnp.bfloat16)
    token_grad = jnp.sum(picked_dx, axis=1).astype(jnp.bfloat16)
    expert_grads = jnp.transpose(grads, (2, 0, 1, 3))
    return (output, token_grad, expert_grads)
```

```python
import functools
import jax
import jax.numpy as jnp
from jax import lax
from jax.experimental import pallas as pl
from jax.experimental.pallas import tpu as pltpu
from jax.sharding import PartitionSpec as P

CAP = 16
F_TILE = 256
VMEM = 58 * 1024 * 1024


def contract(a, b, dims):
    return lax.dot_general(a, b, (dims, ((), ())), preferred_element_type=jnp.float32)


def slot_matrix(routes_t, ids):
    owners = ids.shape[0]
    tok = routes_t.shape[1]
    hit = jnp.zeros((owners, tok), jnp.float32)
    for k in range(routes_t.shape[0]):
        hit = hit + (routes_t[k : k + 1, :] == ids).astype(jnp.float32)
    earlier = (
        lax.broadcasted_iota(jnp.int32, (tok, tok), 0) < lax.broadcasted_iota(jnp.int32, (tok, tok), 1)
    ).astype(jnp.bfloat16)
    rank = contract(hit.astype(jnp.bfloat16), earlier, ((1,), (0,)))
    rank = jnp.where(hit > 0.5, rank, -1.0)
    spread = jnp.broadcast_to(rank[:, None, :], (owners, CAP, tok)).reshape(owners * CAP, tok)
    place = (lax.broadcasted_iota(jnp.int32, (owners * CAP, tok), 0) % CAP).astype(jnp.float32)
    return spread == place


def slot_probs(routes_t, probs_t, ids, chosen):
    owners = ids.shape[0]
    tok = routes_t.shape[1]
    weight = jnp.zeros((owners, tok), jnp.float32)
    for k in range(routes_t.shape[0]):
        weight = weight + jnp.where(routes_t[k : k + 1, :] == ids, probs_t[k : k + 1, :], 0.0)
    spread = jnp.broadcast_to(weight[:, None, :], (owners, CAP, tok)).reshape(owners * CAP, tok)
    return jnp.where(chosen, spread, 0.0)


def dispatch_kernel(routes_ref, probs_ref, ids_ref, tokens_ref, cot_ref, send_ref):
    owners = ids_ref.shape[0]
    chosen = slot_matrix(routes_ref[...], ids_ref[...])
    probs = slot_probs(routes_ref[...], probs_ref[...], ids_ref[...], chosen)
    onehot = chosen.astype(jnp.bfloat16)
    row_prob = jnp.sum(probs, axis=1, keepdims=True)
    width = tokens_ref.shape[1]
    rows = contract(onehot, tokens_ref[...], ((1,), (0,))).astype(jnp.bfloat16)
    send_ref[:, 0] = rows.reshape(owners, CAP, width)
    cot = (row_prob * contract(onehot, cot_ref[...], ((1,), (0,)))).astype(jnp.bfloat16)
    send_ref[:, 1] = cot.reshape(owners, CAP, width)


def dispatch(routes_t, probs_t, ids, tokens, cotangent):
    owners = ids.shape[0]
    width = tokens.shape[1]
    return pl.pallas_call(
        dispatch_kernel,
        out_shape=jax.ShapeDtypeStruct((owners, 2, CAP, width), jnp.bfloat16),
        compiler_params=pltpu.CompilerParams(vmem_limit_bytes=VMEM),
        name="dispatch",
    )(routes_t, probs_t, ids, tokens, cotangent)


def expert_kernel(recv_ref, gate_ref, up_ref, down_ref, grads_ref, back_ref, out_acc, dx_acc):
    step = pl.program_id(0)
    owners, _, cap, width = recv_ref.shape
    rows = recv_ref[:, 0].reshape(owners * cap, width)
    cot = recv_ref[:, 1].reshape(owners * cap, width)
    gate_w, up_w, down_w = gate_ref[...], up_ref[...], down_ref[...]
    gate_pre = contract(rows, gate_w, ((1,), (0,)))
    up_proj = contract(rows, up_w, ((1,), (0,)))
    grad_hidden = contract(cot, down_w, ((1,), (1,)))
    sig = 1.0 / (1.0 + jnp.exp(-gate_pre))
    act = gate_pre * sig
    hidden = (act * up_proj).astype(jnp.bfloat16)
    grad_gate = (grad_hidden * up_proj * sig * (1.0 + gate_pre * (1.0 - sig))).astype(jnp.bfloat16)
    grad_up = (grad_hidden * act).astype(jnp.bfloat16)
    grads_ref[0] = contract(grad_gate, rows, ((0,), (0,))).astype(jnp.bfloat16)
    grads_ref[1] = contract(grad_up, rows, ((0,), (0,))).astype(jnp.bfloat16)
    grads_ref[2] = contract(hidden, cot, ((0,), (0,))).astype(jnp.bfloat16)
    out_part = contract(hidden, down_w, ((1,), (0,)))
    dx_part = contract(grad_gate, gate_w, ((1,), (1,))) + contract(grad_up, up_w, ((1,), (1,)))

    @pl.when(step == 0)
    def _():
        out_acc[...] = out_part
        dx_acc[...] = dx_part

    @pl.when(step > 0)
    def _():
        out_acc[...] += out_part
        dx_acc[...] += dx_part

    @pl.when(step == pl.num_programs(0) - 1)
    def _():
        back_ref[:, 0] = out_acc[...].astype(jnp.bfloat16).reshape(owners, cap, width)
        back_ref[:, 1] = dx_acc[...].astype(jnp.bfloat16).reshape(owners, cap, width)


def expert(recv, gate_weight, up_weight, down_weight, slot):
    owners, _, cap, width = recv.shape
    hidden_units = gate_weight.shape[2]
    rows = owners * cap
    whole = pl.BlockSpec((owners, 2, cap, width), lambda i: (0, 0, 0, 0))
    return pl.pallas_call(
        expert_kernel,
        grid=(hidden_units // F_TILE,),
        in_specs=[
            whole,
            pl.BlockSpec((None, width, F_TILE), lambda i: (slot, 0, i)),
            pl.BlockSpec((None, width, F_TILE), lambda i: (slot, 0, i)),
            pl.BlockSpec((None, F_TILE, width), lambda i: (slot, i, 0)),
        ],
        out_specs=[pl.BlockSpec((3, F_TILE, width), lambda i: (0, i, 0)), whole],
        out_shape=[
            jax.ShapeDtypeStruct((3, hidden_units, width), jnp.bfloat16),
            jax.ShapeDtypeStruct((owners, 2, cap, width), jnp.bfloat16),
        ],
        scratch_shapes=[pltpu.VMEM((rows, width), jnp.float32), pltpu.VMEM((rows, width), jnp.float32)],
        compiler_params=pltpu.CompilerParams(vmem_limit_bytes=VMEM),
        cost_estimate=pl.CostEstimate(
            flops=18 * rows * width * hidden_units,
            bytes_accessed=12 * width * hidden_units + 8 * rows * width,
            transcendentals=rows * hidden_units,
        ),
        name="expert",
    )(recv, gate_weight, up_weight, down_weight)


def combine_kernel(routes_ref, probs_ref, ids0_ref, ids1_ref, back0_ref, back1_ref, output_ref, grad_ref):
    width = output_ref.shape[1]
    output, grad = None, None
    for ids_ref, back_ref in ((ids0_ref, back0_ref), (ids1_ref, back1_ref)):
        rows = ids_ref.shape[0] * CAP
        chosen = slot_matrix(routes_ref[...], ids_ref[...])
        probs = slot_probs(routes_ref[...], probs_ref[...], ids_ref[...], chosen)
        high = probs.astype(jnp.bfloat16)
        low = (probs - high.astype(jnp.float32)).astype(jnp.bfloat16)
        out_rows = back_ref[:, 0].reshape(rows, width)
        dx_rows = back_ref[:, 1].reshape(rows, width)
        one_out = contract(high, out_rows, ((0,), (0,))) + contract(low, out_rows, ((0,), (0,)))
        one_grad = contract(chosen.astype(jnp.bfloat16), dx_rows, ((0,), (0,)))
        output = one_out if output is None else output + one_out
        grad = one_grad if grad is None else grad + one_grad
    output_ref[...] = output.astype(jnp.bfloat16)
    grad_ref[...] = grad.astype(jnp.bfloat16)


def combine(routes_t, probs_t, ids, backs, tok, width):
    row = jax.ShapeDtypeStruct((tok, width), jnp.bfloat16)
    return pl.pallas_call(
        combine_kernel,
        out_shape=[row, row],
        compiler_params=pltpu.CompilerParams(vmem_limit_bytes=VMEM),
        name="combine",
    )(routes_t, probs_t, *ids, *backs)


def shift(value, axis, by):
    n = lax.axis_size(axis)
    return lax.ppermute(value, axis, [(i, (i + by) % n) for i in range(n)])


def add(*terms):
    total = terms[0].astype(jnp.float32)
    for term in terms[1:]:
        total = total + term.astype(jnp.float32)
    return total.astype(jnp.bfloat16)


def sum_over_dp(grads):
    quarter = grads.shape[1] // 4
    half = quarter // 2
    here = lax.axis_index("dp")

    def part(ahead, which):
        start = ((here + ahead) % 4) * quarter + which * half
        return lax.dynamic_slice(grads, (0, start, 0), (3, half, grads.shape[2]))

    far_a = shift(part(2, 0), "dp", 1)
    far_b = shift(part(2, 1), "dp", -1)
    near_b = shift(part(1, 1), "dp", 1)
    near_a = shift(part(3, 0), "dp", -1)
    pair_a = shift(add(part(1, 0), far_a), "dp", 1)
    pair_b = shift(add(part(3, 1), far_b), "dp", -1)
    return add(part(0, 0), near_a, pair_a), add(part(0, 1), near_b, pair_b)


def local(tokens, cotangent, router_probs, routes, partner, gate_weight, up_weight, down_weight):
    tok, width = tokens.shape
    owners = lax.axis_size("expert")
    slots = gate_weight.shape[0]
    routes_t, probs_t = routes.T, router_probs.T
    ids = [(partner * slots + slot).reshape(owners, 1) for slot in range(slots)]
    sends = [dispatch(routes_t, probs_t, ids[slot], tokens, cotangent) for slot in range(slots)]
    grads, backs = [], []
    for slot in range(slots):
        recv = lax.all_to_all(sends[slot], "expert", split_axis=0, concat_axis=0, tiled=True)
        grad, back = expert(recv, gate_weight, up_weight, down_weight, slot)
        grads.append(grad)
        backs.append(lax.all_to_all(back, "expert", split_axis=0, concat_axis=0, tiled=True))
    output, token_grad = combine(routes_t, probs_t, ids, backs, tok, width)
    here = lax.axis_index("expert")
    stays = jnp.sum(jnp.where(jnp.arange(owners) == here, partner, 0)) == here
    finals = []
    for slot in range(slots):
        halves = []
        for part in sum_over_dp(grads[slot]):
            halves.append(jnp.where(stays, part, shift(part, "expert", owners // 2)))
        finals.append(jnp.concatenate(halves, axis=1))
    expert_grads = jnp.stack(finals, axis=0).transpose(2, 0, 1, 3)
    return (output, token_grad, expert_grads)


def solution(mesh):
    rows = P(("expert", "dp"), None)
    by_slot = P("expert", None, None)
    return jax.shard_map(
        local,
        mesh=mesh,
        in_specs=(rows, rows, rows, rows, P(), by_slot, by_slot, by_slot),
        out_specs=(rows, rows, P("dp", "expert", None, None)),
        check_vma=False,
    )
```

```python
import functools
import jax
import jax.numpy as jnp
from jax import lax
from jax.experimental import pallas as pl
from jax.experimental.pallas import tpu as pltpu
from jax.sharding import PartitionSpec as P

CAP = 16
F_TILE = 256
D_TILE = 512
SEND_ORDER = (4, 5, 3, 6, 2, 7, 0, 1)
VMEM = 58 * 1024 * 1024


def contract(a, b, dims):
    return lax.dot_general(a, b, (dims, ((), ())), preferred_element_type=jnp.float32)


def slot_matrix(routes_t, ids):
    owners = ids.shape[0]
    tok = routes_t.shape[1]
    hit = jnp.zeros((owners, tok), jnp.float32)
    for k in range(routes_t.shape[0]):
        hit = hit + (routes_t[k : k + 1, :] == ids).astype(jnp.float32)
    earlier = (
        lax.broadcasted_iota(jnp.int32, (tok, tok), 0) < lax.broadcasted_iota(jnp.int32, (tok, tok), 1)
    ).astype(jnp.bfloat16)
    rank = contract(hit.astype(jnp.bfloat16), earlier, ((1,), (0,)))
    rank = jnp.where(hit > 0.5, rank, -1.0)
    spread = jnp.broadcast_to(rank[:, None, :], (owners, CAP, tok)).reshape(owners * CAP, tok)
    place = (lax.broadcasted_iota(jnp.int32, (owners * CAP, tok), 0) % CAP).astype(jnp.float32)
    return spread == place


def slot_probs(routes_t, probs_t, ids, chosen):
    owners = ids.shape[0]
    tok = routes_t.shape[1]
    weight = jnp.zeros((owners, tok), jnp.float32)
    for k in range(routes_t.shape[0]):
        weight = weight + jnp.where(routes_t[k : k + 1, :] == ids, probs_t[k : k + 1, :], 0.0)
    spread = jnp.broadcast_to(weight[:, None, :], (owners, CAP, tok)).reshape(owners * CAP, tok)
    return jnp.where(chosen, spread, 0.0)


def dispatch_kernel(routes_ref, probs_ref, ids_ref, tokens_ref, cot_ref, send_ref):
    owners = ids_ref.shape[0]
    chosen = slot_matrix(routes_ref[...], ids_ref[...])
    probs = slot_probs(routes_ref[...], probs_ref[...], ids_ref[...], chosen)
    onehot = chosen.astype(jnp.bfloat16)
    row_prob = jnp.sum(probs, axis=1, keepdims=True)
    width = tokens_ref.shape[1]
    rows = contract(onehot, tokens_ref[...], ((1,), (0,))).astype(jnp.bfloat16)
    send_ref[:, 0] = rows.reshape(owners, CAP, width)
    cot = (row_prob * contract(onehot, cot_ref[...], ((1,), (0,)))).astype(jnp.bfloat16)
    send_ref[:, 1] = cot.reshape(owners, CAP, width)


def dispatch(routes_t, probs_t, ids, tokens, cotangent):
    owners = ids.shape[0]
    width = tokens.shape[1]
    return pl.pallas_call(
        dispatch_kernel,
        out_shape=jax.ShapeDtypeStruct((owners, 2, CAP, width), jnp.bfloat16),
        compiler_params=pltpu.CompilerParams(vmem_limit_bytes=VMEM),
        name="dispatch",
    )(routes_t, probs_t, ids, tokens, cotangent)


def expert_kernel(slot, here_ref, recv_ref, gate_hbm, up_hbm, down_hbm, *rest):
    deps, rest = rest[: len(rest) - 20], rest[len(rest) - 20 :]
    del deps
    pieces, back_ref = rest[:8], rest[8]
    (gate_w, up_w, down_w, hidden, grad_pre, hidden_t, gate_t, up_t, grads, load_sem, save_sem) = rest[9:]
    owners, _, cap, width = recv_ref.shape
    units = gate_w.shape[1]
    n_rows = owners * cap
    here = here_ref[0]

    def load(i):
        cols = pl.ds(i * F_TILE, F_TILE)
        return (
            pltpu.make_async_copy(gate_hbm.at[slot, :, cols], gate_w.at[:, cols], load_sem.at[0, i]),
            pltpu.make_async_copy(up_hbm.at[slot, :, cols], up_w.at[:, cols], load_sem.at[1, i]),
            pltpu.make_async_copy(down_hbm.at[slot, cols], down_w.at[cols], load_sem.at[2, i]),
        )

    tiles = units // F_TILE
    for i in range(tiles):
        for copy in load(i):
            copy.start()
    rows = recv_ref[:, 0].reshape(n_rows, width)
    cot = recv_ref[:, 1].reshape(n_rows, width)
    for i in range(tiles):
        for copy in load(i):
            copy.wait()
        cols = pl.ds(i * F_TILE, F_TILE)
        gate_pre = contract(rows, gate_w[:, cols], ((1,), (0,)))
        up_proj = contract(rows, up_w[:, cols], ((1,), (0,)))
        grad_hidden = contract(cot, down_w[cols], ((1,), (1,)))
        sig = 1.0 / (1.0 + jnp.exp(-gate_pre))
        act = gate_pre * sig
        one_hidden = (act * up_proj).astype(jnp.bfloat16)
        one_gate = (grad_hidden * up_proj * sig * (1.0 + gate_pre * (1.0 - sig))).astype(jnp.bfloat16)
        one_up = (grad_hidden * act).astype(jnp.bfloat16)
        hidden[:, cols] = one_hidden
        grad_pre[0, :, cols] = one_gate
        grad_pre[1, :, cols] = one_up
        hidden_t[cols] = one_hidden.T
        gate_t[cols] = one_gate.T
        up_t[cols] = one_up.T

    def grad_chunk(j, carry):
        cols = pl.ds(pl.multiple_of(j * D_TILE, D_TILE), D_TILE)
        for m, (left, second) in enumerate(((gate_t, 0), (up_t, 0), (hidden_t, 1))):
            right = recv_ref[:, second, :, cols].reshape(n_rows, D_TILE)
            grads[m, :, cols] = contract(left[...], right, ((1,), (0,))).astype(jnp.bfloat16)
        return carry

    lax.fori_loop(0, width // D_TILE, grad_chunk, 0)

    quarter = units // 4
    half = quarter // 2

    def save(k):
        start = lax.rem(here + k // 2, 4) * quarter + (k % 2) * half
        source = grads.at[:, pl.ds(pl.multiple_of(start, 32), half), :]
        return pltpu.make_async_copy(source, pieces[k], save_sem.at[k])

    for k in SEND_ORDER:
        save(k).start()

    def back_chunk(j, carry):
        cols = pl.ds(pl.multiple_of(j * D_TILE, D_TILE), D_TILE)
        out = contract(hidden[...], down_w[:, cols], ((1,), (0,)))
        back_ref[:, 0, :, cols] = out.astype(jnp.bfloat16).reshape(owners, cap, D_TILE)
        dx = contract(grad_pre[0], gate_w[cols], ((1,), (1,)))
        dx = dx + contract(grad_pre[1], up_w[cols], ((1,), (1,)))
        back_ref[:, 1, :, cols] = dx.astype(jnp.bfloat16).reshape(owners, cap, D_TILE)
        return carry

    lax.fori_loop(0, width // D_TILE, back_chunk, 0)
    for k in SEND_ORDER:
        save(k).wait()


def expert(slot, here, recv, gate_weight, up_weight, down_weight, deps):
    owners, _, cap, width = recv.shape
    units = gate_weight.shape[2]
    rows = owners * cap
    anywhere = pl.BlockSpec(memory_space=pl.ANY)
    vmem = pl.BlockSpec(memory_space=pltpu.VMEM)
    piece = jax.ShapeDtypeStruct((3, units // 8, width), jnp.bfloat16)
    out = pl.pallas_call(
        functools.partial(expert_kernel, slot),
        in_specs=[pl.BlockSpec(memory_space=pltpu.SMEM), vmem] + [anywhere] * (3 + len(deps)),
        out_specs=[anywhere] * 8 + [vmem],
        out_shape=[piece] * 8 + [jax.ShapeDtypeStruct((owners, 2, cap, width), jnp.bfloat16)],
        scratch_shapes=[
            pltpu.VMEM((width, units), jnp.bfloat16),
            pltpu.VMEM((width, units), jnp.bfloat16),
            pltpu.VMEM((units, width), jnp.bfloat16),
            pltpu.VMEM((rows, units), jnp.bfloat16),
            pltpu.VMEM((2, rows, units), jnp.bfloat16),
            pltpu.VMEM((units, rows), jnp.bfloat16),
            pltpu.VMEM((units, rows), jnp.bfloat16),
            pltpu.VMEM((units, rows), jnp.bfloat16),
            pltpu.VMEM((3, units, width), jnp.bfloat16),
            pltpu.SemaphoreType.DMA((3, units // F_TILE)),
            pltpu.SemaphoreType.DMA((8,)),
        ],
        compiler_params=pltpu.CompilerParams(vmem_limit_bytes=VMEM),
        cost_estimate=pl.CostEstimate(
            flops=18 * rows * width * units,
            bytes_accessed=12 * width * units + 8 * rows * width,
            transcendentals=rows * units,
        ),
        name="expert",
    )(here, recv, gate_weight, up_weight, down_weight, *deps)
    return out[:8], out[8]


def combine_kernel(routes_ref, probs_ref, ids0_ref, ids1_ref, back0_ref, back1_ref, output_ref, grad_ref):
    width = output_ref.shape[1]
    output, grad = None, None
    for ids_ref, back_ref in ((ids0_ref, back0_ref), (ids1_ref, back1_ref)):
        rows = ids_ref.shape[0] * CAP
        chosen = slot_matrix(routes_ref[...], ids_ref[...])
        probs = slot_probs(routes_ref[...], probs_ref[...], ids_ref[...], chosen)
        high = probs.astype(jnp.bfloat16)
        low = (probs - high.astype(jnp.float32)).astype(jnp.bfloat16)
        out_rows = back_ref[:, 0].reshape(rows, width)
        dx_rows = back_ref[:, 1].reshape(rows, width)
        one_out = contract(high, out_rows, ((0,), (0,))) + contract(low, out_rows, ((0,), (0,)))
        one_grad = contract(chosen.astype(jnp.bfloat16), dx_rows, ((0,), (0,)))
        output = one_out if output is None else output + one_out
        grad = one_grad if grad is None else grad + one_grad
    output_ref[...] = output.astype(jnp.bfloat16)
    grad_ref[...] = grad.astype(jnp.bfloat16)


def combine(routes_t, probs_t, ids, backs, tok, width):
    row = jax.ShapeDtypeStruct((tok, width), jnp.bfloat16)
    return pl.pallas_call(
        combine_kernel,
        out_shape=[row, row],
        compiler_params=pltpu.CompilerParams(vmem_limit_bytes=VMEM),
        name="combine",
    )(routes_t, probs_t, *ids, *backs)


def shift(value, axis, by):
    n = lax.axis_size(axis)
    return lax.ppermute(value, axis, [(i, (i + by) % n) for i in range(n)])


def add(*terms):
    total = terms[0].astype(jnp.float32)
    for term in terms[1:]:
        total = total + term.astype(jnp.float32)
    return total.astype(jnp.bfloat16)


def local(tokens, cotangent, router_probs, routes, partner, gate_weight, up_weight, down_weight):
    tok, width = tokens.shape
    owners = lax.axis_size("expert")
    slots = gate_weight.shape[0]
    routes_t, probs_t = routes.T, router_probs.T
    ids = [(partner * slots + slot).reshape(owners, 1) for slot in range(slots)]
    here = lax.axis_index("expert")
    plane = lax.axis_index("dp").reshape(1)
    stays = jnp.sum(jnp.where(jnp.arange(owners) == here, partner, 0)) == here
    sends = [dispatch(routes_t, probs_t, ids[slot], tokens, cotangent) for slot in range(slots)]
    deps = ()
    backs, finals = [], []
    for slot in range(slots):
        recv = lax.all_to_all(sends[slot], "expert", split_axis=0, concat_axis=0, tiled=True)
        pieces, back = expert(slot, plane, recv, gate_weight, up_weight, down_weight, deps)
        backs.append(lax.all_to_all(back, "expert", split_axis=0, concat_axis=0, tiled=True))
        far_a, far_b = shift(pieces[4], "dp", 1), shift(pieces[5], "dp", -1)
        near_b, near_a = shift(pieces[3], "dp", 1), shift(pieces[6], "dp", -1)
        pair_a, pair_b = add(pieces[2], far_a), add(pieces[7], far_b)
        deps = (pair_a, pair_b)
        pair_a, pair_b = shift(pair_a, "dp", 1), shift(pair_b, "dp", -1)
        halves = []
        for part in (add(pieces[0], near_a, pair_a), add(pieces[1], near_b, pair_b)):
            halves.append(jnp.where(stays, part, shift(part, "expert", owners // 2)))
        finals.append(jnp.concatenate(halves, axis=1))
    output, token_grad = combine(routes_t, probs_t, ids, backs, tok, width)
    expert_grads = jnp.stack(finals, axis=0).transpose(2, 0, 1, 3)
    return (output, token_grad, expert_grads)


def solution(mesh):
    rows = P(("expert", "dp"), None)
    by_slot = P("expert", None, None)
    return jax.shard_map(
        local,
        mesh=mesh,
        in_specs=(rows, rows, rows, rows, P(), by_slot, by_slot, by_slot),
        out_specs=(rows, rows, P("dp", "expert", None, None)),
        check_vma=False,
    )
```

```python
import functools
import jax
import jax.numpy as jnp
from jax import lax
from jax.experimental import pallas as pl
from jax.experimental.pallas import tpu as pltpu
from jax.sharding import PartitionSpec as P

CAP = 16
F_TILE = 256
D_TILE = 512
SEND_ORDER = (4, 5, 3, 6, 2, 7, 0, 1)
VMEM = 58 * 1024 * 1024


def contract(a, b, dims):
    return lax.dot_general(a, b, (dims, ((), ())), preferred_element_type=jnp.float32)


def slot_matrix(routes_t, ids):
    owners = ids.shape[0]
    tok = routes_t.shape[1]
    hit = jnp.zeros((owners, tok), jnp.float32)
    for k in range(routes_t.shape[0]):
        hit = hit + (routes_t[k : k + 1, :] == ids).astype(jnp.float32)
    earlier = (
        lax.broadcasted_iota(jnp.int32, (tok, tok), 0) < lax.broadcasted_iota(jnp.int32, (tok, tok), 1)
    ).astype(jnp.bfloat16)
    rank = contract(hit.astype(jnp.bfloat16), earlier, ((1,), (0,)))
    rank = jnp.where(hit > 0.5, rank, -1.0)
    spread = jnp.broadcast_to(rank[:, None, :], (owners, CAP, tok)).reshape(owners * CAP, tok)
    place = (lax.broadcasted_iota(jnp.int32, (owners * CAP, tok), 0) % CAP).astype(jnp.float32)
    return spread == place


def slot_probs(routes_t, probs_t, ids, chosen):
    owners = ids.shape[0]
    tok = routes_t.shape[1]
    weight = jnp.zeros((owners, tok), jnp.float32)
    for k in range(routes_t.shape[0]):
        weight = weight + jnp.where(routes_t[k : k + 1, :] == ids, probs_t[k : k + 1, :], 0.0)
    spread = jnp.broadcast_to(weight[:, None, :], (owners, CAP, tok)).reshape(owners * CAP, tok)
    return jnp.where(chosen, spread, 0.0)


def dispatch_kernel(routes_ref, probs_ref, ids_ref, tokens_ref, cot_ref, send_ref):
    owners = ids_ref.shape[0]
    chosen = slot_matrix(routes_ref[...], ids_ref[...])
    probs = slot_probs(routes_ref[...], probs_ref[...], ids_ref[...], chosen)
    onehot = chosen.astype(jnp.bfloat16)
    row_prob = jnp.sum(probs, axis=1, keepdims=True)
    width = tokens_ref.shape[1]
    rows = contract(onehot, tokens_ref[...], ((1,), (0,))).astype(jnp.bfloat16)
    send_ref[:, 0] = rows.reshape(owners, CAP, width)
    cot = (row_prob * contract(onehot, cot_ref[...], ((1,), (0,)))).astype(jnp.bfloat16)
    send_ref[:, 1] = cot.reshape(owners, CAP, width)


def dispatch(routes_t, probs_t, ids, tokens, cotangent):
    slots, owners, _ = ids.shape
    width = tokens.shape[1]

    def whole(array):
        return pl.BlockSpec(array.shape, lambda i: (0, 0))

    return pl.pallas_call(
        dispatch_kernel,
        grid=(slots,),
        in_specs=[
            whole(routes_t),
            whole(probs_t),
            pl.BlockSpec((None, owners, 1), lambda i: (i, 0, 0)),
            whole(tokens),
            whole(cotangent),
        ],
        out_specs=pl.BlockSpec((owners, 2, CAP, width), lambda i: (0, i, 0, 0)),
        out_shape=jax.ShapeDtypeStruct((owners, 2 * slots, CAP, width), jnp.bfloat16),
        compiler_params=pltpu.CompilerParams(vmem_limit_bytes=VMEM),
        name="dispatch",
    )(routes_t, probs_t, ids, tokens, cotangent)


def expert_kernel(slot, units_of, deps, here_ref, recv_ref, gate_hbm, up_hbm, down_hbm, *rest):
    rest = rest[deps:]
    count = len(units_of)
    ahead, behind, hold, own, back_ref = (
        rest[:count],
        rest[count : 2 * count],
        rest[2 * count : 3 * count],
        rest[3 * count : 4 * count],
        rest[4 * count],
    )
    (gate_w, up_w, down_w, hidden, grad_pre, hidden_t, gate_t, up_t, grads, load_sem, save_sem) = rest[4 * count + 1 :]
    place_of = {m: (u, at) for u, group in enumerate(units_of) for at, m in enumerate(group)}
    owners, _, cap, width = recv_ref.shape
    units = gate_w.shape[1]
    n_rows = owners * cap
    here = here_ref[0]

    def load(i):
        cols = pl.ds(i * F_TILE, F_TILE)
        return (
            pltpu.make_async_copy(gate_hbm.at[slot, :, cols], gate_w.at[:, cols], load_sem.at[0, i]),
            pltpu.make_async_copy(up_hbm.at[slot, :, cols], up_w.at[:, cols], load_sem.at[1, i]),
            pltpu.make_async_copy(down_hbm.at[slot, cols], down_w.at[cols], load_sem.at[2, i]),
        )

    tiles = units // F_TILE
    for i in range(tiles):
        for copy in load(i):
            copy.start()
    rows = recv_ref[:, 0].reshape(n_rows, width)
    cot = recv_ref[:, 1].reshape(n_rows, width)
    for i in range(tiles):
        for copy in load(i):
            copy.wait()
        cols = pl.ds(i * F_TILE, F_TILE)
        gate_pre = contract(rows, gate_w[:, cols], ((1,), (0,)))
        up_proj = contract(rows, up_w[:, cols], ((1,), (0,)))
        grad_hidden = contract(cot, down_w[cols], ((1,), (1,)))
        sig = 1.0 / (1.0 + jnp.exp(-gate_pre))
        act = gate_pre * sig
        one_hidden = (act * up_proj).astype(jnp.bfloat16)
        one_gate = (grad_hidden * up_proj * sig * (1.0 + gate_pre * (1.0 - sig))).astype(jnp.bfloat16)
        one_up = (grad_hidden * act).astype(jnp.bfloat16)
        hidden[:, cols] = one_hidden
        grad_pre[0, :, cols] = one_gate
        grad_pre[1, :, cols] = one_up
        hidden_t[cols] = one_hidden.T
        gate_t[cols] = one_gate.T
        up_t[cols] = one_up.T

    quarter = units // 4
    half = quarter // 2

    def save(m, k):
        start = lax.rem(here + k // 2, 4) * quarter + (k % 2) * half
        source = grads.at[m, pl.ds(pl.multiple_of(start, 32), half), :]
        u, at = place_of[m]
        target = (
            own[u].at[at, pl.ds(0, half)],
            own[u].at[at, pl.ds(half, half)],
            hold[u].at[0, at],
            ahead[u].at[1, at],
            ahead[u].at[0, at],
            behind[u].at[0, at],
            behind[u].at[1, at],
            hold[u].at[1, at],
        )[k]
        return pltpu.make_async_copy(source, target, save_sem.at[m, k])

    for m, (left, second) in enumerate(((gate_t, 0), (up_t, 0), (hidden_t, 1))):

        def grad_chunk(j, carry, m=m, left=left, second=second):
            cols = pl.ds(pl.multiple_of(j * D_TILE, D_TILE), D_TILE)
            right = recv_ref[:, second, :, cols].reshape(n_rows, D_TILE)
            grads[m, :, cols] = contract(left[...], right, ((1,), (0,))).astype(jnp.bfloat16)
            return carry

        lax.fori_loop(0, width // D_TILE, grad_chunk, 0)
        for k in SEND_ORDER:
            save(m, k).start()

    def back_chunk(j, carry):
        cols = pl.ds(pl.multiple_of(j * D_TILE, D_TILE), D_TILE)
        out = contract(hidden[...], down_w[:, cols], ((1,), (0,)))
        back_ref[:, 0, :, cols] = out.astype(jnp.bfloat16).reshape(owners, cap, D_TILE)
        dx = contract(grad_pre[0], gate_w[cols], ((1,), (1,)))
        dx = dx + contract(grad_pre[1], up_w[cols], ((1,), (1,)))
        back_ref[:, 1, :, cols] = dx.astype(jnp.bfloat16).reshape(owners, cap, D_TILE)
        return carry

    lax.fori_loop(0, width // D_TILE, back_chunk, 0)
    for m in range(3):
        for k in SEND_ORDER:
            save(m, k).wait()


def expert(slot, units_of, here, recv, gate_weight, up_weight, down_weight, deps):
    owners, _, cap, width = recv.shape
    units = gate_weight.shape[2]
    rows = owners * cap
    half = units // 8
    anywhere = pl.BlockSpec(memory_space=pl.ANY)
    given = pl.BlockSpec((owners, 2, cap, width), lambda i: (0, slot, 0, 0))
    back = pl.BlockSpec((owners, 2, cap, width), lambda i: (0, 0, 0, 0))
    count = len(units_of)
    shapes = [(2, len(group), half, width) for group in units_of] * 3
    shapes += [(len(group), 2 * half, width) for group in units_of] + [(owners, 2, cap, width)]
    out = pl.pallas_call(
        functools.partial(expert_kernel, slot, units_of, len(deps)),
        grid=(1,),
        in_specs=[pl.BlockSpec(memory_space=pltpu.SMEM), given] + [anywhere] * (3 + len(deps)),
        out_specs=[anywhere] * (4 * count) + [back],
        out_shape=[jax.ShapeDtypeStruct(shape, jnp.bfloat16) for shape in shapes],
        scratch_shapes=[
            pltpu.VMEM((width, units), jnp.bfloat16),
            pltpu.VMEM((width, units), jnp.bfloat16),
            pltpu.VMEM((units, width), jnp.bfloat16),
            pltpu.VMEM((rows, units), jnp.bfloat16),
            pltpu.VMEM((2, rows, units), jnp.bfloat16),
            pltpu.VMEM((units, rows), jnp.bfloat16),
            pltpu.VMEM((units, rows), jnp.bfloat16),
            pltpu.VMEM((units, rows), jnp.bfloat16),
            pltpu.VMEM((3, units, width), jnp.bfloat16),
            pltpu.SemaphoreType.DMA((3, units // F_TILE)),
            pltpu.SemaphoreType.DMA((3, 8)),
        ],
        compiler_params=pltpu.CompilerParams(vmem_limit_bytes=VMEM),
        cost_estimate=pl.CostEstimate(
            flops=40 * rows * width * units,
            bytes_accessed=12 * width * units + 8 * rows * width,
            transcendentals=rows * units,
        ),
        name="expert",
    )(here, recv, gate_weight, up_weight, down_weight, *deps)
    return tuple(out[i * count : (i + 1) * count] for i in range(4)) + (out[4 * count],)


def combine_kernel(routes_ref, probs_ref, ids0_ref, ids1_ref, back0_ref, back1_ref, output_ref, grad_ref):
    width = output_ref.shape[1]
    output, grad = None, None
    for ids_ref, back_ref in ((ids0_ref, back0_ref), (ids1_ref, back1_ref)):
        rows = ids_ref.shape[0] * CAP
        chosen = slot_matrix(routes_ref[...], ids_ref[...])
        probs = slot_probs(routes_ref[...], probs_ref[...], ids_ref[...], chosen)
        high = probs.astype(jnp.bfloat16)
        low = (probs - high.astype(jnp.float32)).astype(jnp.bfloat16)
        out_rows = back_ref[:, 0].reshape(rows, width)
        dx_rows = back_ref[:, 1].reshape(rows, width)
        one_out = contract(high, out_rows, ((0,), (0,))) + contract(low, out_rows, ((0,), (0,)))
        one_grad = contract(chosen.astype(jnp.bfloat16), dx_rows, ((0,), (0,)))
        output = one_out if output is None else output + one_out
        grad = one_grad if grad is None else grad + one_grad
    output_ref[...] = output.astype(jnp.bfloat16)
    grad_ref[...] = grad.astype(jnp.bfloat16)


def combine(routes_t, probs_t, ids, backs, tok, width):
    row = jax.ShapeDtypeStruct((tok, width), jnp.bfloat16)
    return pl.pallas_call(
        combine_kernel,
        out_shape=[row, row],
        compiler_params=pltpu.CompilerParams(vmem_limit_bytes=VMEM),
        name="combine",
    )(routes_t, probs_t, *ids, *backs)


def shift(value, axis, by):
    n = lax.axis_size(axis)
    return lax.ppermute(value, axis, [(i, (i + by) % n) for i in range(n)])


def add(*terms):
    total = terms[0].astype(jnp.float32)
    for term in terms[1:]:
        total = total + term.astype(jnp.float32)
    return total.astype(jnp.bfloat16)


def spread_call(kernel, name, count, inputs, out_shapes, deps):
    specs = []
    for array, at in inputs:
        rows, width = array.shape[-2:]
        if at is None:
            specs.append(pl.BlockSpec((1, rows, width), lambda i: (i, 0, 0)))
        else:
            specs.append(pl.BlockSpec((1, 1, rows, width), functools.partial(lambda at, i: (at, i, 0, 0), at)))
    size = sum(shape[0] * shape[1] for shape in out_shapes)
    return pl.pallas_call(
        kernel,
        grid=(count,),
        in_specs=specs + [pl.BlockSpec(memory_space=pl.ANY)] * len(deps),
        out_specs=[pl.BlockSpec((1, *shape), lambda i: (i, 0, 0)) for shape in out_shapes],
        out_shape=[jax.ShapeDtypeStruct((count, *shape), jnp.bfloat16) for shape in out_shapes],
        compiler_params=pltpu.CompilerParams(vmem_limit_bytes=VMEM),
        cost_estimate=pl.CostEstimate(flops=2 * count * size, bytes_accessed=6 * count * size, transcendentals=0),
        name=name,
    )(*(array for array, _ in inputs), *deps)


def pair_kernel(hold_a_ref, hold_b_ref, far_a_ref, far_b_ref, *rest):
    pair_a_ref, pair_b_ref = rest[-2:]
    pair_a_ref[0] = add(hold_a_ref[0, 0], far_a_ref[0, 0])
    pair_b_ref[0] = add(hold_b_ref[0, 0], far_b_ref[0, 0])


def pair(hold, from_behind, from_ahead, deps):
    _, count, half, width = hold.shape
    inputs = [(hold, 0), (hold, 1), (from_behind, 0), (from_ahead, 0)]
    return spread_call(pair_kernel, "pair", count, inputs, [(half, width)] * 2, deps)


def finish_kernel(own_ref, near_a_ref, near_b_ref, pair_a_ref, pair_b_ref, *rest):
    sum_ref = rest[-1]
    half = pair_a_ref.shape[1]
    sum_ref[0, :half] = add(own_ref[0, :half], near_a_ref[0, 0], pair_a_ref[0])
    sum_ref[0, half:] = add(own_ref[0, half:], near_b_ref[0, 0], pair_b_ref[0])


def finish(own, from_behind, from_ahead, pair_a, pair_b, deps):
    count, quarter, width = own.shape
    inputs = [(own, None), (from_ahead, 1), (from_behind, 1), (pair_a, None), (pair_b, None)]
    return spread_call(finish_kernel, "finish", count, inputs, [(quarter, width)], deps)[0]


def place_kernel(stays_ref, own0_ref, other0_ref, own1_ref, other1_ref, *rest):
    out_ref = rest[-1]
    stays = stays_ref[0] == 1
    out_ref[:, 0, 0, :] = jnp.where(stays, own0_ref[0], other0_ref[0])
    out_ref[:, 0, 1, :] = jnp.where(stays, own1_ref[0], other1_ref[0])


def place(m, stays, parts, so_far, deps):
    _, quarter, width = parts[0][0].shape
    specs = [pl.BlockSpec((1, quarter, width), functools.partial(lambda at, i: (at, 0, 0), at)) for _, at in parts]
    given = ([] if so_far is None else [so_far]) + list(deps)
    return pl.pallas_call(
        place_kernel,
        grid=(1,),
        in_specs=[pl.BlockSpec(memory_space=pltpu.SMEM)] + specs + [pl.BlockSpec(memory_space=pl.ANY)] * len(given),
        out_specs=pl.BlockSpec((quarter, 1, 2, width), lambda i: (0, m, 0, 0)),
        out_shape=jax.ShapeDtypeStruct((quarter, 3, 2, width), jnp.bfloat16),
        input_output_aliases={} if so_far is None else {5: 0},
        compiler_params=pltpu.CompilerParams(vmem_limit_bytes=VMEM),
        cost_estimate=pl.CostEstimate(flops=2 * quarter * width, bytes_accessed=12 * quarter * width, transcendentals=0),
        name="place",
    )(stays, *(array for array, _ in parts), *given)


GROUPS = (((0, 1, 2),), ((0,), (1,), (2,)))


def local(tokens, cotangent, router_probs, routes, partner, gate_weight, up_weight, down_weight):
    tok, width = tokens.shape
    owners = lax.axis_size("expert")
    slots = gate_weight.shape[0]
    routes_t, probs_t = routes.T, router_probs.T
    ids = (partner[None, :] * slots + jnp.arange(slots, dtype=jnp.int32)[:, None]).reshape(slots, owners, 1)
    here = lax.axis_index("expert")
    plane = lax.axis_index("dp").reshape(1)
    stays = (jnp.sum(jnp.where(jnp.arange(owners) == here, partner, 0)) == here).astype(jnp.int32).reshape(1)
    send = dispatch(routes_t, probs_t, ids, tokens, cotangent)
    recv = lax.all_to_all(send, "expert", split_axis=0, concat_axis=0, tiled=True)
    backs, final = [], {}
    for slot in range(slots):
        groups = GROUPS[slot]
        ahead, behind, hold, own, back = expert(slot, groups, plane, recv, gate_weight, up_weight, down_weight, ())
        backs.append(lax.all_to_all(back, "expert", split_axis=0, concat_axis=0, tiled=True))
        from_behind = [shift(piece, "dp", 1) for piece in ahead]
        from_ahead = [shift(piece, "dp", -1) for piece in behind]
        for u, group in enumerate(groups):
            pair_a, pair_b = pair(hold[u], from_behind[u], from_ahead[u], ())
            pair_a, pair_b = shift(pair_a, "dp", 1), shift(pair_b, "dp", -1)
            total = finish(own[u], from_behind[u], from_ahead[u], pair_a, pair_b, ())
            other = shift(total, "expert", owners // 2)
            for at, m in enumerate(group):
                final[slot, m] = [(total, at), (other, at)]
    output, token_grad = combine(routes_t, probs_t, (ids[0], ids[1]), backs, tok, width)
    grads = None
    for m in range(3):
        deps = (output,) if m == 2 else ()
        grads = place(m, stays, final[0, m] + final[1, m], grads, deps)
    return (output, token_grad, grads.transpose(0, 2, 1, 3))


def solution(mesh):
    rows = P(("expert", "dp"), None)
    by_slot = P("expert", None, None)
    return jax.shard_map(
        local,
        mesh=mesh,
        in_specs=(rows, rows, rows, rows, P(), by_slot, by_slot, by_slot),
        out_specs=(rows, rows, P("dp", "expert", None, None)),
        check_vma=False,
    )
```

```python
import functools
import jax
import jax.numpy as jnp
from jax import lax
from jax.experimental import pallas as pl
from jax.experimental.pallas import tpu as pltpu
from jax.sharding import PartitionSpec as P

CAP = 16
TOPK = 6
F_TILE = 256
D_TILE = 512
SEND_ORDER = (4, 5, 3, 6, 2, 7, 0, 1)
VMEM = 58 * 1024 * 1024


def contract(a, b, dims):
    return lax.dot_general(a, b, (dims, ((), ())), preferred_element_type=jnp.float32)


def slot_matrix(routes, ids):
    n = ids.shape[0]
    tok = routes.shape[1]
    hit = jnp.zeros((n, tok), jnp.float32)
    for k in range(routes.shape[0]):
        hit = hit + (routes[k : k + 1, :] == ids).astype(jnp.float32)
    earlier = (
        lax.broadcasted_iota(jnp.int32, (tok, tok), 0) < lax.broadcasted_iota(jnp.int32, (tok, tok), 1)
    ).astype(jnp.bfloat16)
    rank = contract(hit.astype(jnp.bfloat16), earlier, ((1,), (0,)))
    rank = jnp.where(hit > 0.5, rank, -1.0)
    spread = jnp.broadcast_to(rank[:, None, :], (n, CAP, tok)).reshape(n * CAP, tok)
    place = (lax.broadcasted_iota(jnp.int32, (n * CAP, tok), 0) % CAP).astype(jnp.float32)
    return spread == place


def slot_probs(routes, probs, ids, chosen):
    n = ids.shape[0]
    tok = routes.shape[1]
    weight = jnp.zeros((n, tok), jnp.float32)
    for k in range(routes.shape[0]):
        weight = weight + jnp.where(routes[k : k + 1, :] == ids, probs[k : k + 1, :], 0.0)
    spread = jnp.broadcast_to(weight[:, None, :], (n, CAP, tok)).reshape(n * CAP, tok)
    return jnp.where(chosen, spread, 0.0)


def dispatch_kernel(ids_ref, *rest):
    send_ref = rest[-1]
    n = ids_ref.shape[0]
    for source in range(2):
        meta_ref, tokens_ref, cot_ref = rest[3 * source : 3 * source + 3]
        routes, probs = meta_ref[:TOPK], meta_ref[TOPK : 2 * TOPK]
        width = tokens_ref.shape[1]
        chosen = slot_matrix(routes, ids_ref[...])
        row_prob = jnp.sum(slot_probs(routes, probs, ids_ref[...], chosen), axis=1, keepdims=True)
        onehot = chosen.astype(jnp.bfloat16)
        rows = contract(onehot, tokens_ref[...], ((1,), (0,))).astype(jnp.bfloat16)
        send_ref[:, source, 0] = rows.reshape(n, CAP, width)
        cot = (row_prob * contract(onehot, cot_ref[...], ((1,), (0,)))).astype(jnp.bfloat16)
        send_ref[:, source, 1] = cot.reshape(n, CAP, width)


def dispatch(ids, sources):
    slots, n, _ = ids.shape
    width = sources[0][1].shape[1]
    arrays = [array for source in sources for array in source]
    return pl.pallas_call(
        dispatch_kernel,
        grid=(slots,),
        in_specs=[pl.BlockSpec((None, n, 1), lambda i: (i, 0, 0))]
        + [pl.BlockSpec(array.shape, lambda i: (0, 0)) for array in arrays],
        out_specs=pl.BlockSpec((n, None, 2, 2, CAP, width), lambda i: (0, i, 0, 0, 0, 0)),
        out_shape=jax.ShapeDtypeStruct((n, slots, 2, 2, CAP, width), jnp.bfloat16),
        compiler_params=pltpu.CompilerParams(vmem_limit_bytes=VMEM),
        name="dispatch",
    )(ids, *arrays)


def expert_kernel(slot, units_of, deps, here_ref, recv_ref, gate_hbm, up_hbm, down_hbm, *rest):
    rest = rest[deps:]
    count = len(units_of)
    ahead, behind, hold, own, back_ref = (
        rest[:count],
        rest[count : 2 * count],
        rest[2 * count : 3 * count],
        rest[3 * count : 4 * count],
        rest[4 * count],
    )
    (gate_w, up_w, down_w, hidden, grad_pre, hidden_t, gate_t, up_t, grads, load_sem, save_sem) = rest[4 * count + 1 :]
    place_of = {m: (u, at) for u, group in enumerate(units_of) for at, m in enumerate(group)}
    n, _, _, cap, width = recv_ref.shape
    units = gate_w.shape[1]
    n_rows = n * 2 * cap
    here = here_ref[0]

    def load(i):
        cols = pl.ds(i * F_TILE, F_TILE)
        return (
            pltpu.make_async_copy(gate_hbm.at[slot, :, cols], gate_w.at[:, cols], load_sem.at[0, i]),
            pltpu.make_async_copy(up_hbm.at[slot, :, cols], up_w.at[:, cols], load_sem.at[1, i]),
            pltpu.make_async_copy(down_hbm.at[slot, cols], down_w.at[cols], load_sem.at[2, i]),
        )

    tiles = units // F_TILE
    for i in range(tiles):
        for copy in load(i):
            copy.start()
    rows = recv_ref[:, :, 0].reshape(n_rows, width)
    cot = recv_ref[:, :, 1].reshape(n_rows, width)
    for i in range(tiles):
        for copy in load(i):
            copy.wait()
        cols = pl.ds(i * F_TILE, F_TILE)
        gate_pre = contract(rows, gate_w[:, cols], ((1,), (0,)))
        up_proj = contract(rows, up_w[:, cols], ((1,), (0,)))
        grad_hidden = contract(cot, down_w[cols], ((1,), (1,)))
        sig = 1.0 / (1.0 + jnp.exp(-gate_pre))
        act = gate_pre * sig
        one_hidden = (act * up_proj).astype(jnp.bfloat16)
        one_gate = (grad_hidden * up_proj * sig * (1.0 + gate_pre * (1.0 - sig))).astype(jnp.bfloat16)
        one_up = (grad_hidden * act).astype(jnp.bfloat16)
        hidden[:, cols] = one_hidden
        grad_pre[0, :, cols] = one_gate
        grad_pre[1, :, cols] = one_up
        hidden_t[cols] = one_hidden.T
        gate_t[cols] = one_gate.T
        up_t[cols] = one_up.T

    quarter = units // 4
    half = quarter // 2

    def save(m, k):
        start = lax.rem(here + k // 2, 4) * quarter + (k % 2) * half
        source = grads.at[m, pl.ds(pl.multiple_of(start, 32), half), :]
        u, at = place_of[m]
        target = (
            own[u].at[at, pl.ds(0, half)],
            own[u].at[at, pl.ds(half, half)],
            hold[u].at[0, at],
            ahead[u].at[1, at],
            ahead[u].at[0, at],
            behind[u].at[0, at],
            behind[u].at[1, at],
            hold[u].at[1, at],
        )[k]
        return pltpu.make_async_copy(source, target, save_sem.at[m, k])

    for m, (left, second) in enumerate(((gate_t, 0), (up_t, 0), (hidden_t, 1))):

        def grad_chunk(j, carry, m=m, left=left, second=second):
            cols = pl.ds(pl.multiple_of(j * D_TILE, D_TILE), D_TILE)
            right = recv_ref[:, :, second, :, cols].reshape(n_rows, D_TILE)
            grads[m, :, cols] = contract(left[...], right, ((1,), (0,))).astype(jnp.bfloat16)
            return carry

        lax.fori_loop(0, width // D_TILE, grad_chunk, 0)
        for k in SEND_ORDER:
            save(m, k).start()

    def back_chunk(j, carry):
        cols = pl.ds(pl.multiple_of(j * D_TILE, D_TILE), D_TILE)
        out = contract(hidden[...], down_w[:, cols], ((1,), (0,)))
        back_ref[:, :, 0, :, cols] = out.astype(jnp.bfloat16).reshape(n, 2, cap, D_TILE)
        dx = contract(grad_pre[0], gate_w[cols], ((1,), (1,)))
        dx = dx + contract(grad_pre[1], up_w[cols], ((1,), (1,)))
        back_ref[:, :, 1, :, cols] = dx.astype(jnp.bfloat16).reshape(n, 2, cap, D_TILE)
        return carry

    lax.fori_loop(0, width // D_TILE, back_chunk, 0)
    for m in range(3):
        for k in SEND_ORDER:
            save(m, k).wait()


def expert(slot, units_of, here, recv, gate_weight, up_weight, down_weight, deps):
    n, _, _, _, cap, width = recv.shape
    units = gate_weight.shape[2]
    rows = n * 2 * cap
    half = units // 8
    anywhere = pl.BlockSpec(memory_space=pl.ANY)
    given = pl.BlockSpec((n, None, 2, 2, cap, width), lambda i: (0, slot, 0, 0, 0, 0))
    back = pl.BlockSpec((n, 2, 2, cap, width), lambda i: (0, 0, 0, 0, 0))
    count = len(units_of)
    shapes = [(2, len(group), half, width) for group in units_of] * 3
    shapes += [(len(group), 2 * half, width) for group in units_of] + [(n, 2, 2, cap, width)]
    out = pl.pallas_call(
        functools.partial(expert_kernel, slot, units_of, len(deps)),
        grid=(1,),
        in_specs=[pl.BlockSpec(memory_space=pltpu.SMEM), given] + [anywhere] * (3 + len(deps)),
        out_specs=[anywhere] * (4 * count) + [back],
        out_shape=[jax.ShapeDtypeStruct(shape, jnp.bfloat16) for shape in shapes],
        scratch_shapes=[
            pltpu.VMEM((width, units), jnp.bfloat16),
            pltpu.VMEM((width, units), jnp.bfloat16),
            pltpu.VMEM((units, width), jnp.bfloat16),
            pltpu.VMEM((rows, units), jnp.bfloat16),
            pltpu.VMEM((2, rows, units), jnp.bfloat16),
            pltpu.VMEM((units, rows), jnp.bfloat16),
            pltpu.VMEM((units, rows), jnp.bfloat16),
            pltpu.VMEM((units, rows), jnp.bfloat16),
            pltpu.VMEM((3, units, width), jnp.bfloat16),
            pltpu.SemaphoreType.DMA((3, units // F_TILE)),
            pltpu.SemaphoreType.DMA((3, 8)),
        ],
        compiler_params=pltpu.CompilerParams(vmem_limit_bytes=VMEM),
        cost_estimate=pl.CostEstimate(
            flops=40 * rows * width * units,
            bytes_accessed=12 * width * units + 8 * rows * width,
            transcendentals=rows * units,
        ),
        name="expert",
    )(here, recv, gate_weight, up_weight, down_weight, *deps)
    return tuple(out[i * count : (i + 1) * count] for i in range(4)) + (out[4 * count],)


def combine_kernel(ids_ref, meta0_ref, meta1_ref, back0_ref, back1_ref, output_ref, grad_ref, other_ref):
    width = output_ref.shape[1]
    for source, meta_ref in enumerate((meta0_ref, meta1_ref)):
        routes, probs = meta_ref[:TOPK], meta_ref[TOPK : 2 * TOPK]
        output, grad = None, None
        for slot, back_ref in enumerate((back0_ref, back1_ref)):
            ids = ids_ref[slot]
            rows = ids.shape[0] * CAP
            chosen = slot_matrix(routes, ids)
            weight = slot_probs(routes, probs, ids, chosen)
            high = weight.astype(jnp.bfloat16)
            low = (weight - high.astype(jnp.float32)).astype(jnp.bfloat16)
            out_rows = back_ref[:, source, 0].reshape(rows, width)
            dx_rows = back_ref[:, source, 1].reshape(rows, width)
            one_out = contract(high, out_rows, ((0,), (0,))) + contract(low, out_rows, ((0,), (0,)))
            one_grad = contract(chosen.astype(jnp.bfloat16), dx_rows, ((0,), (0,)))
            output = one_out if output is None else output + one_out
            grad = one_grad if grad is None else grad + one_grad
        if source == 0:
            output_ref[...] = output
            grad_ref[...] = grad
        else:
            other_ref[0] = output.astype(jnp.bfloat16)
            other_ref[1] = grad.astype(jnp.bfloat16)


def combine(ids, metas, backs, tok, width):
    row = jax.ShapeDtypeStruct((tok, width), jnp.float32)
    return pl.pallas_call(
        combine_kernel,
        out_shape=[row, row, jax.ShapeDtypeStruct((2, tok, width), jnp.bfloat16)],
        compiler_params=pltpu.CompilerParams(vmem_limit_bytes=VMEM),
        name="combine",
    )(ids, *metas, *backs)


def shift(value, axis, by):
    n = lax.axis_size(axis)
    return lax.ppermute(value, axis, [(i, (i + by) % n) for i in range(n)])


def add(*terms):
    total = terms[0].astype(jnp.float32)
    for term in terms[1:]:
        total = total + term.astype(jnp.float32)
    return total.astype(jnp.bfloat16)


def spread_call(kernel, name, count, inputs, out_shapes, deps):
    specs = []
    for array, at in inputs:
        rows, width = array.shape[-2:]
        if at is None:
            specs.append(pl.BlockSpec((1, rows, width), lambda i: (i, 0, 0)))
        else:
            specs.append(pl.BlockSpec((1, 1, rows, width), functools.partial(lambda at, i: (at, i, 0, 0), at)))
    size = sum(shape[0] * shape[1] for shape in out_shapes)
    return pl.pallas_call(
        kernel,
        grid=(count,),
        in_specs=specs + [pl.BlockSpec(memory_space=pl.ANY)] * len(deps),
        out_specs=[pl.BlockSpec((1, *shape), lambda i: (i, 0, 0)) for shape in out_shapes],
        out_shape=[jax.ShapeDtypeStruct((count, *shape), jnp.bfloat16) for shape in out_shapes],
        compiler_params=pltpu.CompilerParams(vmem_limit_bytes=VMEM),
        cost_estimate=pl.CostEstimate(flops=2 * count * size, bytes_accessed=6 * count * size, transcendentals=0),
        name=name,
    )(*(array for array, _ in inputs), *deps)


def pair_kernel(hold_a_ref, hold_b_ref, far_a_ref, far_b_ref, *rest):
    pair_a_ref, pair_b_ref = rest[-2:]
    pair_a_ref[0] = add(hold_a_ref[0, 0], far_a_ref[0, 0])
    pair_b_ref[0] = add(hold_b_ref[0, 0], far_b_ref[0, 0])


def pair(hold, from_behind, from_ahead, deps):
    _, count, half, width = hold.shape
    inputs = [(hold, 0), (hold, 1), (from_behind, 0), (from_ahead, 0)]
    return spread_call(pair_kernel, "pair", count, inputs, [(half, width)] * 2, deps)


def finish_kernel(own_ref, near_a_ref, near_b_ref, pair_a_ref, pair_b_ref, *rest):
    sum_ref = rest[-1]
    half = pair_a_ref.shape[1]
    sum_ref[0, :half] = add(own_ref[0, :half], near_a_ref[0, 0], pair_a_ref[0])
    sum_ref[0, half:] = add(own_ref[0, half:], near_b_ref[0, 0], pair_b_ref[0])


def finish(own, from_behind, from_ahead, pair_a, pair_b, deps):
    count, quarter, width = own.shape
    inputs = [(own, None), (from_ahead, 1), (from_behind, 1), (pair_a, None), (pair_b, None)]
    return spread_call(finish_kernel, "finish", count, inputs, [(quarter, width)], deps)[0]


def place_kernel(stays_ref, own0_ref, other0_ref, own1_ref, other1_ref, *rest):
    out_ref = rest[-1]
    stays = stays_ref[0] == 1
    out_ref[:, 0, 0, :] = jnp.where(stays, own0_ref[0], other0_ref[0])
    out_ref[:, 0, 1, :] = jnp.where(stays, own1_ref[0], other1_ref[0])


def place(m, stays, parts, so_far, deps):
    _, quarter, width = parts[0][0].shape
    specs = [pl.BlockSpec((1, quarter, width), functools.partial(lambda at, i: (at, 0, 0), at)) for _, at in parts]
    given = ([] if so_far is None else [so_far]) + list(deps)
    return pl.pallas_call(
        place_kernel,
        grid=(1,),
        in_specs=[pl.BlockSpec(memory_space=pltpu.SMEM)] + specs + [pl.BlockSpec(memory_space=pl.ANY)] * len(given),
        out_specs=pl.BlockSpec((quarter, 1, 2, width), lambda i: (0, m, 0, 0)),
        out_shape=jax.ShapeDtypeStruct((quarter, 3, 2, width), jnp.bfloat16),
        input_output_aliases={} if so_far is None else {5: 0},
        compiler_params=pltpu.CompilerParams(vmem_limit_bytes=VMEM),
        cost_estimate=pl.CostEstimate(flops=2 * quarter * width, bytes_accessed=12 * quarter * width, transcendentals=0),
        name="place",
    )(stays, *(array for array, _ in parts), *given)


GROUPS = (((0, 1, 2),), ((0,), (1,), (2,)))


def swap_cores(value):
    return lax.ppermute(value, "core", [(0, 1), (1, 0)])


def local(tokens, cotangent, router_probs, routes, partner, gate_weight, up_weight, down_weight):
    tok, width = tokens.shape
    slots = gate_weight.shape[0]
    core = lax.axis_index("core")
    owner = (lax.axis_index("x") * lax.axis_size("y") + lax.axis_index("y")) * 2 + core
    plane = lax.axis_index("dp").reshape(1)
    stays = (jnp.sum(jnp.where(jnp.arange(partner.shape[0]) == owner, partner, 0)) == owner).astype(jnp.int32).reshape(1)
    held = jnp.where(core == 0, partner[0::2], partner[1::2])
    ids = held[None, :] * slots + jnp.arange(slots, dtype=jnp.int32)[:, None]
    ids = ids.astype(jnp.float32).reshape(slots, -1, 1)
    meta = jnp.concatenate([routes.T.astype(jnp.float32), router_probs.T], axis=0)
    sources = [(meta, tokens, cotangent), (swap_cores(meta), swap_cores(tokens), swap_cores(cotangent))]
    send = dispatch(ids, sources)
    recv = lax.all_to_all(send, ("x", "y"), split_axis=0, concat_axis=0, tiled=True)
    backs, final, first_pair = [], {}, None
    for slot in range(slots):
        groups = GROUPS[slot]
        ahead, behind, hold, own, back = expert(slot, groups, plane, recv, gate_weight, up_weight, down_weight, ())
        from_behind = [shift(piece, "dp", 1) for piece in ahead]
        from_ahead = [shift(piece, "dp", -1) for piece in behind]
        if first_pair is not None:
            back, _ = lax.optimization_barrier((back, first_pair))
        backs.append(lax.all_to_all(back, ("x", "y"), split_axis=0, concat_axis=0, tiled=True))
        for u, group in enumerate(groups):
            pair_a, pair_b = pair(hold[u], from_behind[u], from_ahead[u], ())
            if first_pair is None:
                first_pair = pair_a
            pair_a, pair_b = shift(pair_a, "dp", 1), shift(pair_b, "dp", -1)
            total = finish(own[u], from_behind[u], from_ahead[u], pair_a, pair_b, ())
            other = shift(total, "x", 2)
            for at, m in enumerate(group):
                final[slot, m] = [(total, at), (other, at)]
    output, token_grad, other = combine(ids, (sources[0][0], sources[1][0]), backs, tok, width)
    other = swap_cores(other)
    output, token_grad = add(output, other[0]), add(token_grad, other[1])
    grads = None
    for m in range(3):
        deps = (output,) if m == 2 else ()
        grads = place(m, stays, final[0, m] + final[1, m], grads, deps)
    return (output, token_grad, grads.transpose(0, 2, 1, 3))


def solution(mesh):
    devices = mesh.devices
    grid = jax.sharding.Mesh(devices.reshape(4, 4, 2, devices.shape[1]), ("x", "y", "core", "dp"))
    rows = P(("x", "y", "core", "dp"), None)
    by_slot = P(("x", "y", "core"), None, None)
    return jax.shard_map(
        local,
        mesh=grid,
        in_specs=(rows, rows, rows, rows, P(), by_slot, by_slot, by_slot),
        out_specs=(rows, rows, P("dp", ("x", "y", "core"), None, None)),
        check_vma=False,
    )
```

```python
import functools
import jax
import jax.numpy as jnp
from jax import lax
from jax.experimental import pallas as pl
from jax.experimental.pallas import tpu as pltpu
from jax.sharding import PartitionSpec as P

CAP = 16
F_TILE = 256
D_TILE = 512
SEND_ORDER = (4, 5, 3, 6, 2, 7, 0, 1)
VMEM = 58 * 1024 * 1024


def contract(a, b, dims):
    return lax.dot_general(a, b, (dims, ((), ())), preferred_element_type=jnp.float32)


def slot_matrix(routes_t, ids):
    owners = ids.shape[0]
    tok = routes_t.shape[1]
    hit = jnp.zeros((owners, tok), jnp.float32)
    for k in range(routes_t.shape[0]):
        hit = hit + (routes_t[k : k + 1, :] == ids).astype(jnp.float32)
    earlier = (
        lax.broadcasted_iota(jnp.int32, (tok, tok), 0) < lax.broadcasted_iota(jnp.int32, (tok, tok), 1)
    ).astype(jnp.bfloat16)
    rank = contract(hit.astype(jnp.bfloat16), earlier, ((1,), (0,)))
    rank = jnp.where(hit > 0.5, rank, -1.0)
    spread = jnp.broadcast_to(rank[:, None, :], (owners, CAP, tok)).reshape(owners * CAP, tok)
    place = (lax.broadcasted_iota(jnp.int32, (owners * CAP, tok), 0) % CAP).astype(jnp.float32)
    return spread == place


def slot_probs(routes_t, probs_t, ids, chosen):
    owners = ids.shape[0]
    tok = routes_t.shape[1]
    weight = jnp.zeros((owners, tok), jnp.float32)
    for k in range(routes_t.shape[0]):
        weight = weight + jnp.where(routes_t[k : k + 1, :] == ids, probs_t[k : k + 1, :], 0.0)
    spread = jnp.broadcast_to(weight[:, None, :], (owners, CAP, tok)).reshape(owners * CAP, tok)
    return jnp.where(chosen, spread, 0.0)


def dispatch_kernel(routes_ref, probs_ref, ids_ref, tokens_ref, cot_ref, *rest):
    send_ref = rest[-1]
    owners = ids_ref.shape[0]
    chosen = slot_matrix(routes_ref[...], ids_ref[...])
    probs = slot_probs(routes_ref[...], probs_ref[...], ids_ref[...], chosen)
    onehot = chosen.astype(jnp.bfloat16)
    row_prob = jnp.sum(probs, axis=1, keepdims=True)
    width = tokens_ref.shape[1]
    rows = contract(onehot, tokens_ref[...], ((1,), (0,))).astype(jnp.bfloat16)
    send_ref[:, 0] = rows.reshape(owners, CAP, width)
    cot = (row_prob * contract(onehot, cot_ref[...], ((1,), (0,)))).astype(jnp.bfloat16)
    send_ref[:, 1] = cot.reshape(owners, CAP, width)


def dispatch(routes_t, probs_t, ids, tokens, cotangent, deps):
    slots, owners, _ = ids.shape
    width = tokens.shape[1]

    def whole(array):
        return pl.BlockSpec(array.shape, lambda i: (0, 0))

    return pl.pallas_call(
        dispatch_kernel,
        grid=(slots,),
        in_specs=[
            whole(routes_t),
            whole(probs_t),
            pl.BlockSpec((None, owners, 1), lambda i: (i, 0, 0)),
            whole(tokens),
            whole(cotangent),
        ]
        + [pl.BlockSpec(memory_space=pl.ANY)] * len(deps),
        out_specs=pl.BlockSpec((owners, 2, CAP, width), lambda i: (0, i, 0, 0)),
        out_shape=jax.ShapeDtypeStruct((owners, 2 * slots, CAP, width), jnp.bfloat16),
        compiler_params=pltpu.CompilerParams(vmem_limit_bytes=VMEM),
        name="dispatch",
    )(routes_t, probs_t, ids, tokens, cotangent, *deps)


def expert_kernel(slot, units_of, deps, here_ref, recv_ref, gate_hbm, up_hbm, down_hbm, *rest):
    rest = rest[deps:]
    count = len(units_of)
    ahead, behind, hold, own, back_ref = (
        rest[:count],
        rest[count : 2 * count],
        rest[2 * count : 3 * count],
        rest[3 * count : 4 * count],
        rest[4 * count],
    )
    (gate_w, up_w, down_w, hidden, grad_pre, hidden_t, gate_t, up_t, grads, load_sem, save_sem) = rest[4 * count + 1 :]
    place_of = {m: (u, at) for u, group in enumerate(units_of) for at, m in enumerate(group)}
    owners, _, cap, width = recv_ref.shape
    units = gate_w.shape[1]
    n_rows = owners * cap
    here = here_ref[0]

    def load(i):
        cols = pl.ds(i * F_TILE, F_TILE)
        return (
            pltpu.make_async_copy(gate_hbm.at[slot, :, cols], gate_w.at[:, cols], load_sem.at[0, i]),
            pltpu.make_async_copy(up_hbm.at[slot, :, cols], up_w.at[:, cols], load_sem.at[1, i]),
            pltpu.make_async_copy(down_hbm.at[slot, cols], down_w.at[cols], load_sem.at[2, i]),
        )

    tiles = units // F_TILE
    for i in range(tiles):
        for copy in load(i):
            copy.start()
    rows = recv_ref[:, 0].reshape(n_rows, width)
    cot = recv_ref[:, 1].reshape(n_rows, width)
    for i in range(tiles):
        for copy in load(i):
            copy.wait()
        cols = pl.ds(i * F_TILE, F_TILE)
        gate_pre = contract(rows, gate_w[:, cols], ((1,), (0,)))
        up_proj = contract(rows, up_w[:, cols], ((1,), (0,)))
        grad_hidden = contract(cot, down_w[cols], ((1,), (1,)))
        sig = 1.0 / (1.0 + jnp.exp(-gate_pre))
        act = gate_pre * sig
        one_hidden = (act * up_proj).astype(jnp.bfloat16)
        one_gate = (grad_hidden * up_proj * sig * (1.0 + gate_pre * (1.0 - sig))).astype(jnp.bfloat16)
        one_up = (grad_hidden * act).astype(jnp.bfloat16)
        hidden[:, cols] = one_hidden
        grad_pre[0, :, cols] = one_gate
        grad_pre[1, :, cols] = one_up
        hidden_t[cols] = one_hidden.T
        gate_t[cols] = one_gate.T
        up_t[cols] = one_up.T

    quarter = units // 4
    half = quarter // 2

    def save(m, k):
        start = lax.rem(here + k // 2, 4) * quarter + (k % 2) * half
        source = grads.at[m, pl.ds(pl.multiple_of(start, 32), half), :]
        u, at = place_of[m]
        target = (
            own[u].at[at, pl.ds(0, half)],
            own[u].at[at, pl.ds(half, half)],
            hold[u].at[0, at],
            ahead[u].at[1, at],
            ahead[u].at[0, at],
            behind[u].at[0, at],
            behind[u].at[1, at],
            hold[u].at[1, at],
        )[k]
        return pltpu.make_async_copy(source, target, save_sem.at[m, k])

    for m, (left, second) in enumerate(((gate_t, 0), (up_t, 0), (hidden_t, 1))):

        def grad_chunk(j, carry, m=m, left=left, second=second):
            cols = pl.ds(pl.multiple_of(j * D_TILE, D_TILE), D_TILE)
            right = recv_ref[:, second, :, cols].reshape(n_rows, D_TILE)
            grads[m, :, cols] = contract(left[...], right, ((1,), (0,))).astype(jnp.bfloat16)
            return carry

        lax.fori_loop(0, width // D_TILE, grad_chunk, 0)
        for k in SEND_ORDER:
            save(m, k).start()

    def back_chunk(j, carry):
        cols = pl.ds(pl.multiple_of(j * D_TILE, D_TILE), D_TILE)
        out = contract(hidden[...], down_w[:, cols], ((1,), (0,)))
        back_ref[:, 0, :, cols] = out.astype(jnp.bfloat16).reshape(owners, cap, D_TILE)
        dx = contract(grad_pre[0], gate_w[cols], ((1,), (1,)))
        dx = dx + contract(grad_pre[1], up_w[cols], ((1,), (1,)))
        back_ref[:, 1, :, cols] = dx.astype(jnp.bfloat16).reshape(owners, cap, D_TILE)
        return carry

    lax.fori_loop(0, width // D_TILE, back_chunk, 0)
    for m in range(3):
        for k in SEND_ORDER:
            save(m, k).wait()


def expert(slot, units_of, here, recv, gate_weight, up_weight, down_weight, deps):
    owners, _, cap, width = recv.shape
    units = gate_weight.shape[2]
    rows = owners * cap
    half = units // 8
    anywhere = pl.BlockSpec(memory_space=pl.ANY)
    given = pl.BlockSpec((owners, 2, cap, width), lambda i: (0, slot, 0, 0))
    back = pl.BlockSpec((owners, 2, cap, width), lambda i: (0, 0, 0, 0))
    count = len(units_of)
    shapes = [(2, len(group), half, width) for group in units_of] * 3
    shapes += [(len(group), 2 * half, width) for group in units_of] + [(owners, 2, cap, width)]
    out = pl.pallas_call(
        functools.partial(expert_kernel, slot, units_of, len(deps)),
        grid=(1,),
        in_specs=[pl.BlockSpec(memory_space=pltpu.SMEM), given] + [anywhere] * (3 + len(deps)),
        out_specs=[anywhere] * (4 * count) + [back],
        out_shape=[jax.ShapeDtypeStruct(shape, jnp.bfloat16) for shape in shapes],
        scratch_shapes=[
            pltpu.VMEM((width, units), jnp.bfloat16),
            pltpu.VMEM((width, units), jnp.bfloat16),
            pltpu.VMEM((units, width), jnp.bfloat16),
            pltpu.VMEM((rows, units), jnp.bfloat16),
            pltpu.VMEM((2, rows, units), jnp.bfloat16),
            pltpu.VMEM((units, rows), jnp.bfloat16),
            pltpu.VMEM((units, rows), jnp.bfloat16),
            pltpu.VMEM((units, rows), jnp.bfloat16),
            pltpu.VMEM((3, units, width), jnp.bfloat16),
            pltpu.SemaphoreType.DMA((3, units // F_TILE)),
            pltpu.SemaphoreType.DMA((3, 8)),
        ],
        compiler_params=pltpu.CompilerParams(vmem_limit_bytes=VMEM),
        cost_estimate=pl.CostEstimate(
            flops=40 * rows * width * units,
            bytes_accessed=12 * width * units + 8 * rows * width,
            transcendentals=rows * units,
        ),
        name="expert",
    )(here, recv, gate_weight, up_weight, down_weight, *deps)
    return tuple(out[i * count : (i + 1) * count] for i in range(4)) + (out[4 * count],)


def combine_kernel(routes_ref, probs_ref, ids0_ref, ids1_ref, back0_ref, back1_ref, output_ref, grad_ref):
    width = output_ref.shape[1]
    output, grad = None, None
    for ids_ref, back_ref in ((ids0_ref, back0_ref), (ids1_ref, back1_ref)):
        rows = ids_ref.shape[0] * CAP
        chosen = slot_matrix(routes_ref[...], ids_ref[...])
        probs = slot_probs(routes_ref[...], probs_ref[...], ids_ref[...], chosen)
        high = probs.astype(jnp.bfloat16)
        low = (probs - high.astype(jnp.float32)).astype(jnp.bfloat16)
        out_rows = back_ref[:, 0].reshape(rows, width)
        dx_rows = back_ref[:, 1].reshape(rows, width)
        one_out = contract(high, out_rows, ((0,), (0,))) + contract(low, out_rows, ((0,), (0,)))
        one_grad = contract(chosen.astype(jnp.bfloat16), dx_rows, ((0,), (0,)))
        output = one_out if output is None else output + one_out
        grad = one_grad if grad is None else grad + one_grad
    output_ref[...] = output.astype(jnp.bfloat16)
    grad_ref[...] = grad.astype(jnp.bfloat16)


def combine(routes_t, probs_t, ids, backs, tok, width):
    row = jax.ShapeDtypeStruct((tok, width), jnp.bfloat16)
    return pl.pallas_call(
        combine_kernel,
        out_shape=[row, row],
        compiler_params=pltpu.CompilerParams(vmem_limit_bytes=VMEM),
        name="combine",
    )(routes_t, probs_t, *ids, *backs)


def shift(value, axis, by):
    n = lax.axis_size(axis)
    return lax.ppermute(value, axis, [(i, (i + by) % n) for i in range(n)])


def add(*terms):
    total = terms[0].astype(jnp.float32)
    for term in terms[1:]:
        total = total + term.astype(jnp.float32)
    return total.astype(jnp.bfloat16)


def spread_call(kernel, name, count, inputs, out_shapes, deps):
    specs = []
    for array, at in inputs:
        rows, width = array.shape[-2:]
        if at is None:
            specs.append(pl.BlockSpec((1, rows, width), lambda i: (i, 0, 0)))
        else:
            specs.append(pl.BlockSpec((1, 1, rows, width), functools.partial(lambda at, i: (at, i, 0, 0), at)))
    size = sum(shape[0] * shape[1] for shape in out_shapes)
    return pl.pallas_call(
        kernel,
        grid=(count,),
        in_specs=specs + [pl.BlockSpec(memory_space=pl.ANY)] * len(deps),
        out_specs=[pl.BlockSpec((1, *shape), lambda i: (i, 0, 0)) for shape in out_shapes],
        out_shape=[jax.ShapeDtypeStruct((count, *shape), jnp.bfloat16) for shape in out_shapes],
        compiler_params=pltpu.CompilerParams(vmem_limit_bytes=VMEM),
        cost_estimate=pl.CostEstimate(flops=2 * count * size, bytes_accessed=6 * count * size, transcendentals=0),
        name=name,
    )(*(array for array, _ in inputs), *deps)


def pair_kernel(hold_a_ref, hold_b_ref, far_a_ref, far_b_ref, *rest):
    pair_a_ref, pair_b_ref = rest[-2:]
    pair_a_ref[0] = add(hold_a_ref[0, 0], far_a_ref[0, 0])
    pair_b_ref[0] = add(hold_b_ref[0, 0], far_b_ref[0, 0])


def pair(hold, from_behind, from_ahead, deps):
    _, count, half, width = hold.shape
    inputs = [(hold, 0), (hold, 1), (from_behind, 0), (from_ahead, 0)]
    return spread_call(pair_kernel, "pair", count, inputs, [(half, width)] * 2, deps)


def finish_kernel(own_ref, near_a_ref, near_b_ref, pair_a_ref, pair_b_ref, *rest):
    sum_ref = rest[-1]
    half = pair_a_ref.shape[1]
    sum_ref[0, :half] = add(own_ref[0, :half], near_a_ref[0, 0], pair_a_ref[0])
    sum_ref[0, half:] = add(own_ref[0, half:], near_b_ref[0, 0], pair_b_ref[0])


def finish(own, from_behind, from_ahead, pair_a, pair_b, deps):
    count, quarter, width = own.shape
    inputs = [(own, None), (from_ahead, 1), (from_behind, 1), (pair_a, None), (pair_b, None)]
    return spread_call(finish_kernel, "finish", count, inputs, [(quarter, width)], deps)[0]


def place_kernel(stays_ref, own0_ref, other0_ref, own1_ref, other1_ref, *rest):
    out_ref = rest[-1]
    stays = stays_ref[0] == 1
    out_ref[:, 0, 0, :] = jnp.where(stays, own0_ref[0], other0_ref[0])
    out_ref[:, 0, 1, :] = jnp.where(stays, own1_ref[0], other1_ref[0])


def place(m, stays, parts, so_far, deps):
    _, quarter, width = parts[0][0].shape
    specs = [pl.BlockSpec((1, quarter, width), functools.partial(lambda at, i: (at, 0, 0), at)) for _, at in parts]
    given = ([] if so_far is None else [so_far]) + list(deps)
    return pl.pallas_call(
        place_kernel,
        grid=(1,),
        in_specs=[pl.BlockSpec(memory_space=pltpu.SMEM)] + specs + [pl.BlockSpec(memory_space=pl.ANY)] * len(given),
        out_specs=pl.BlockSpec((quarter, 1, 2, width), lambda i: (0, m, 0, 0)),
        out_shape=jax.ShapeDtypeStruct((quarter, 3, 2, width), jnp.bfloat16),
        input_output_aliases={} if so_far is None else {5: 0},
        compiler_params=pltpu.CompilerParams(vmem_limit_bytes=VMEM),
        cost_estimate=pl.CostEstimate(flops=2 * quarter * width, bytes_accessed=12 * quarter * width, transcendentals=0),
        name="place",
    )(stays, *(array for array, _ in parts), *given)


GROUPS = (((0, 1, 2),), ((0,), (1,), (2,)))


def local(tokens, cotangent, router_probs, routes, partner, gate_weight, up_weight, down_weight):
    tok, width = tokens.shape
    owners = lax.axis_size("expert")
    slots = gate_weight.shape[0]
    routes_t, probs_t = routes.T, router_probs.T
    ids = (partner[None, :] * slots + jnp.arange(slots, dtype=jnp.int32)[:, None]).reshape(slots, owners, 1)
    here = lax.axis_index("expert")
    plane = lax.axis_index("dp").reshape(1)
    stays = (jnp.sum(jnp.where(jnp.arange(owners) == here, partner, 0)) == here).astype(jnp.int32).reshape(1)
    send = dispatch(routes_t, probs_t, ids, tokens, cotangent, (plane, stays))
    recv = lax.all_to_all(send, "expert", split_axis=0, concat_axis=0, tiled=True)
    backs, final = [], {}
    for slot in range(slots):
        groups = GROUPS[slot]
        ahead, behind, hold, own, back = expert(slot, groups, plane, recv, gate_weight, up_weight, down_weight, ())
        backs.append(lax.all_to_all(back, "expert", split_axis=0, concat_axis=0, tiled=True))
        from_behind = [shift(piece, "dp", 1) for piece in ahead]
        from_ahead = [shift(piece, "dp", -1) for piece in behind]
        totals = []
        for u, group in enumerate(groups):
            after = (totals[u - 2],) if u >= 2 else ()
            pair_a, pair_b = pair(hold[u], from_behind[u], from_ahead[u], after)
            pair_a, pair_b = shift(pair_a, "dp", 1), shift(pair_b, "dp", -1)
            total = finish(own[u], from_behind[u], from_ahead[u], pair_a, pair_b, ())
            totals.append(total)
            other = shift(total, "expert", owners // 2)
            for at, m in enumerate(group):
                final[slot, m] = [(total, at), (other, at)]
    output, token_grad = combine(routes_t, probs_t, (ids[0], ids[1]), backs, tok, width)
    grads = None
    for m in range(3):
        deps = (output,) if m == 2 else ()
        grads = place(m, stays, final[0, m] + final[1, m], grads, deps)
    return (output, token_grad, grads.transpose(0, 2, 1, 3))


def solution(mesh):
    rows = P(("expert", "dp"), None)
    by_slot = P("expert", None, None)
    return jax.shard_map(
        local,
        mesh=mesh,
        in_specs=(rows, rows, rows, rows, P(), by_slot, by_slot, by_slot),
        out_specs=(rows, rows, P("dp", "expert", None, None)),
        check_vma=False,
    )
```

```python
import functools
import jax
import jax.numpy as jnp
from jax import lax
from jax.experimental import pallas as pl
from jax.experimental.pallas import tpu as pltpu
from jax.sharding import PartitionSpec as P

CAP = 16
F_TILE = 256
D_TILE = 2048
SEND_ORDER = (4, 5, 3, 6, 2, 7, 0, 1)
VMEM = 58 * 1024 * 1024


def contract(a, b, dims):
    return lax.dot_general(a, b, (dims, ((), ())), preferred_element_type=jnp.float32)


def slot_matrix(routes_t, ids):
    owners = ids.shape[0]
    tok = routes_t.shape[1]
    hit = jnp.zeros((owners, tok), jnp.float32)
    for k in range(routes_t.shape[0]):
        hit = hit + (routes_t[k : k + 1, :] == ids).astype(jnp.float32)
    earlier = (
        lax.broadcasted_iota(jnp.int32, (tok, tok), 0) < lax.broadcasted_iota(jnp.int32, (tok, tok), 1)
    ).astype(jnp.bfloat16)
    rank = contract(hit.astype(jnp.bfloat16), earlier, ((1,), (0,)))
    rank = jnp.where(hit > 0.5, rank, -1.0)
    spread = jnp.broadcast_to(rank[:, None, :], (owners, CAP, tok)).reshape(owners * CAP, tok)
    place = (lax.broadcasted_iota(jnp.int32, (owners * CAP, tok), 0) % CAP).astype(jnp.float32)
    return spread == place


def slot_probs(routes_t, probs_t, ids, chosen):
    owners = ids.shape[0]
    tok = routes_t.shape[1]
    weight = jnp.zeros((owners, tok), jnp.float32)
    for k in range(routes_t.shape[0]):
        weight = weight + jnp.where(routes_t[k : k + 1, :] == ids, probs_t[k : k + 1, :], 0.0)
    spread = jnp.broadcast_to(weight[:, None, :], (owners, CAP, tok)).reshape(owners * CAP, tok)
    return jnp.where(chosen, spread, 0.0)


def dispatch_kernel(routes_ref, probs_ref, ids_ref, tokens_ref, cot_ref, *rest):
    slots, owners, _ = ids_ref.shape
    width = tokens_ref.shape[1]
    for slot, send_ref in enumerate(rest[len(rest) - slots :]):
        chosen = slot_matrix(routes_ref[...], ids_ref[slot])
        probs = slot_probs(routes_ref[...], probs_ref[...], ids_ref[slot], chosen)
        onehot = chosen.astype(jnp.bfloat16)
        row_prob = jnp.sum(probs, axis=1, keepdims=True)
        rows = contract(onehot, tokens_ref[...], ((1,), (0,))).astype(jnp.bfloat16)
        send_ref[:, 0] = rows.reshape(owners, CAP, width)
        cot = (row_prob * contract(onehot, cot_ref[...], ((1,), (0,)))).astype(jnp.bfloat16)
        send_ref[:, 1] = cot.reshape(owners, CAP, width)


def dispatch(routes_t, probs_t, ids, tokens, cotangent, deps):
    slots, owners, _ = ids.shape
    width = tokens.shape[1]
    vmem = pl.BlockSpec(memory_space=pltpu.VMEM)
    return pl.pallas_call(
        dispatch_kernel,
        in_specs=[vmem] * 5 + [pl.BlockSpec(memory_space=pl.ANY)] * len(deps),
        out_shape=[jax.ShapeDtypeStruct((owners, 2, CAP, width), jnp.bfloat16)] * slots,
        compiler_params=pltpu.CompilerParams(vmem_limit_bytes=VMEM),
        name="dispatch",
    )(routes_t, probs_t, ids, tokens, cotangent, *deps)


def expert_kernel(slot, units_of, deps, here_ref, recv_ref, gate_hbm, up_hbm, down_hbm, *rest):
    rest = rest[deps:]
    count = len(units_of)
    ahead, behind, hold, own, back_ref = (
        rest[:count],
        rest[count : 2 * count],
        rest[2 * count : 3 * count],
        rest[3 * count : 4 * count],
        rest[4 * count],
    )
    (gate_w, up_w, down_w, hidden, grad_pre, hidden_t, gate_t, up_t, grads, load_sem, save_sem) = rest[4 * count + 1 :]
    place_of = {m: (u, at) for u, group in enumerate(units_of) for at, m in enumerate(group)}
    owners, _, cap, width = recv_ref.shape
    units = gate_w.shape[1]
    n_rows = owners * cap
    here = here_ref[0]

    def load(i):
        cols = pl.ds(i * F_TILE, F_TILE)
        return (
            pltpu.make_async_copy(gate_hbm.at[slot, :, cols], gate_w.at[:, cols], load_sem.at[0, i]),
            pltpu.make_async_copy(up_hbm.at[slot, :, cols], up_w.at[:, cols], load_sem.at[1, i]),
            pltpu.make_async_copy(down_hbm.at[slot, cols], down_w.at[cols], load_sem.at[2, i]),
        )

    tiles = units // F_TILE
    for i in range(tiles):
        for copy in load(i):
            copy.start()
    rows = recv_ref[:, 0].reshape(n_rows, width)
    cot = recv_ref[:, 1].reshape(n_rows, width)
    for i in range(tiles):
        for copy in load(i):
            copy.wait()
        cols = pl.ds(i * F_TILE, F_TILE)
        gate_pre = contract(rows, gate_w[:, cols], ((1,), (0,)))
        up_proj = contract(rows, up_w[:, cols], ((1,), (0,)))
        grad_hidden = contract(cot, down_w[cols], ((1,), (1,)))
        sig = 1.0 / (1.0 + jnp.exp(-gate_pre))
        act = gate_pre * sig
        one_hidden = (act * up_proj).astype(jnp.bfloat16)
        one_gate = (grad_hidden * up_proj * sig * (1.0 + gate_pre * (1.0 - sig))).astype(jnp.bfloat16)
        one_up = (grad_hidden * act).astype(jnp.bfloat16)
        hidden[:, cols] = one_hidden
        grad_pre[0, :, cols] = one_gate
        grad_pre[1, :, cols] = one_up
        hidden_t[cols] = one_hidden.T
        gate_t[cols] = one_gate.T
        up_t[cols] = one_up.T

    quarter = units // 4
    half = quarter // 2

    def save(m, k):
        start = lax.rem(here + k // 2, 4) * quarter + (k % 2) * half
        source = grads.at[m, pl.ds(pl.multiple_of(start, 32), half), :]
        u, at = place_of[m]
        target = (
            own[u].at[at, pl.ds(0, half)],
            own[u].at[at, pl.ds(half, half)],
            hold[u].at[0, at],
            ahead[u].at[1, at],
            ahead[u].at[0, at],
            behind[u].at[0, at],
            behind[u].at[1, at],
            hold[u].at[1, at],
        )[k]
        return pltpu.make_async_copy(source, target, save_sem.at[m, k])

    for m, (left, second) in enumerate(((gate_t, 0), (up_t, 0), (hidden_t, 1))):

        def grad_chunk(j, carry, m=m, left=left, second=second):
            cols = pl.ds(pl.multiple_of(j * D_TILE, D_TILE), D_TILE)
            right = recv_ref[:, second, :, cols].reshape(n_rows, D_TILE)
            grads[m, :, cols] = contract(left[...], right, ((1,), (0,))).astype(jnp.bfloat16)
            return carry

        lax.fori_loop(0, width // D_TILE, grad_chunk, 0)
        for k in SEND_ORDER:
            save(m, k).start()

    def back_chunk(j, carry):
        cols = pl.ds(pl.multiple_of(j * D_TILE, D_TILE), D_TILE)
        out = contract(hidden[...], down_w[:, cols], ((1,), (0,)))
        back_ref[:, 0, :, cols] = out.astype(jnp.bfloat16).reshape(owners, cap, D_TILE)
        dx = contract(grad_pre[0], gate_w[cols], ((1,), (1,)))
        dx = dx + contract(grad_pre[1], up_w[cols], ((1,), (1,)))
        back_ref[:, 1, :, cols] = dx.astype(jnp.bfloat16).reshape(owners, cap, D_TILE)
        return carry

    lax.fori_loop(0, width // D_TILE, back_chunk, 0)
    for m in range(3):
        for k in SEND_ORDER:
            save(m, k).wait()


def expert(slot, units_of, here, recv, gate_weight, up_weight, down_weight, deps):
    owners, _, cap, width = recv.shape
    units = gate_weight.shape[2]
    rows = owners * cap
    half = units // 8
    anywhere = pl.BlockSpec(memory_space=pl.ANY)
    given = pl.BlockSpec((owners, 2, cap, width), lambda i: (0, 0, 0, 0))
    back = pl.BlockSpec((owners, 2, cap, width), lambda i: (0, 0, 0, 0))
    count = len(units_of)
    shapes = [(2, len(group), half, width) for group in units_of] * 3
    shapes += [(len(group), 2 * half, width) for group in units_of] + [(owners, 2, cap, width)]
    out = pl.pallas_call(
        functools.partial(expert_kernel, slot, units_of, len(deps)),
        grid=(1,),
        in_specs=[pl.BlockSpec(memory_space=pltpu.SMEM), given] + [anywhere] * (3 + len(deps)),
        out_specs=[anywhere] * (4 * count) + [back],
        out_shape=[jax.ShapeDtypeStruct(shape, jnp.bfloat16) for shape in shapes],
        scratch_shapes=[
            pltpu.VMEM((width, units), jnp.bfloat16),
            pltpu.VMEM((width, units), jnp.bfloat16),
            pltpu.VMEM((units, width), jnp.bfloat16),
            pltpu.VMEM((rows, units), jnp.bfloat16),
            pltpu.VMEM((2, rows, units), jnp.bfloat16),
            pltpu.VMEM((units, rows), jnp.bfloat16),
            pltpu.VMEM((units, rows), jnp.bfloat16),
            pltpu.VMEM((units, rows), jnp.bfloat16),
            pltpu.VMEM((3, units, width), jnp.bfloat16),
            pltpu.SemaphoreType.DMA((3, units // F_TILE)),
            pltpu.SemaphoreType.DMA((3, 8)),
        ],
        compiler_params=pltpu.CompilerParams(vmem_limit_bytes=VMEM),
        cost_estimate=pl.CostEstimate(
            flops=40 * rows * width * units,
            bytes_accessed=12 * width * units + 8 * rows * width,
            transcendentals=rows * units,
        ),
        name="expert",
    )(here, recv, gate_weight, up_weight, down_weight, *deps)
    return tuple(out[i * count : (i + 1) * count] for i in range(4)) + (out[4 * count],)


def combine_kernel(routes_ref, probs_ref, ids0_ref, ids1_ref, back0_ref, back1_ref, output_ref, grad_ref):
    width = output_ref.shape[1]
    output, grad = None, None
    for ids_ref, back_ref in ((ids0_ref, back0_ref), (ids1_ref, back1_ref)):
        rows = ids_ref.shape[0] * CAP
        chosen = slot_matrix(routes_ref[...], ids_ref[...])
        probs = slot_probs(routes_ref[...], probs_ref[...], ids_ref[...], chosen)
        high = probs.astype(jnp.bfloat16)
        low = (probs - high.astype(jnp.float32)).astype(jnp.bfloat16)
        out_rows = back_ref[:, 0].reshape(rows, width)
        dx_rows = back_ref[:, 1].reshape(rows, width)
        one_out = contract(high, out_rows, ((0,), (0,))) + contract(low, out_rows, ((0,), (0,)))
        one_grad = contract(chosen.astype(jnp.bfloat16), dx_rows, ((0,), (0,)))
        output = one_out if output is None else output + one_out
        grad = one_grad if grad is None else grad + one_grad
    output_ref[...] = output.astype(jnp.bfloat16)
    grad_ref[...] = grad.astype(jnp.bfloat16)


def combine(routes_t, probs_t, ids, backs, tok, width):
    row = jax.ShapeDtypeStruct((tok, width), jnp.bfloat16)
    return pl.pallas_call(
        combine_kernel,
        out_shape=[row, row],
        compiler_params=pltpu.CompilerParams(vmem_limit_bytes=VMEM),
        name="combine",
    )(routes_t, probs_t, *ids, *backs)


def shift(value, axis, by):
    n = lax.axis_size(axis)
    return lax.ppermute(value, axis, [(i, (i + by) % n) for i in range(n)])


def add(*terms):
    total = terms[0].astype(jnp.float32)
    for term in terms[1:]:
        total = total + term.astype(jnp.float32)
    return total.astype(jnp.bfloat16)


def spread_call(kernel, name, count, inputs, out_shapes, deps):
    specs = []
    for array, at in inputs:
        rows, width = array.shape[-2:]
        if at is None:
            specs.append(pl.BlockSpec((1, rows, width), lambda i: (i, 0, 0)))
        else:
            specs.append(pl.BlockSpec((1, 1, rows, width), functools.partial(lambda at, i: (at, i, 0, 0), at)))
    size = sum(shape[0] * shape[1] for shape in out_shapes)
    return pl.pallas_call(
        kernel,
        grid=(count,),
        in_specs=specs + [pl.BlockSpec(memory_space=pl.ANY)] * len(deps),
        out_specs=[pl.BlockSpec((1, *shape), lambda i: (i, 0, 0)) for shape in out_shapes],
        out_shape=[jax.ShapeDtypeStruct((count, *shape), jnp.bfloat16) for shape in out_shapes],
        compiler_params=pltpu.CompilerParams(vmem_limit_bytes=VMEM),
        cost_estimate=pl.CostEstimate(flops=2 * count * size, bytes_accessed=6 * count * size, transcendentals=0),
        name=name,
    )(*(array for array, _ in inputs), *deps)


def pair_kernel(hold_a_ref, hold_b_ref, far_a_ref, far_b_ref, *rest):
    pair_a_ref, pair_b_ref = rest[-2:]
    pair_a_ref[0] = add(hold_a_ref[0, 0], far_a_ref[0, 0])
    pair_b_ref[0] = add(hold_b_ref[0, 0], far_b_ref[0, 0])


def pair(hold, from_behind, from_ahead, deps):
    _, count, half, width = hold.shape
    inputs = [(hold, 0), (hold, 1), (from_behind, 0), (from_ahead, 0)]
    return spread_call(pair_kernel, "pair", count, inputs, [(half, width)] * 2, deps)


def finish_kernel(own_ref, near_a_ref, near_b_ref, pair_a_ref, pair_b_ref, *rest):
    sum_ref = rest[-1]
    half = pair_a_ref.shape[1]
    sum_ref[0, :half] = add(own_ref[0, :half], near_a_ref[0, 0], pair_a_ref[0])
    sum_ref[0, half:] = add(own_ref[0, half:], near_b_ref[0, 0], pair_b_ref[0])


def finish(own, from_behind, from_ahead, pair_a, pair_b, deps):
    count, quarter, width = own.shape
    inputs = [(own, None), (from_ahead, 1), (from_behind, 1), (pair_a, None), (pair_b, None)]
    return spread_call(finish_kernel, "finish", count, inputs, [(quarter, width)], deps)[0]


def place_kernel(stays_ref, own0_ref, other0_ref, own1_ref, other1_ref, *rest):
    out_ref = rest[-1]
    stays = stays_ref[0] == 1
    out_ref[:, 0, 0, :] = jnp.where(stays, own0_ref[0], other0_ref[0])
    out_ref[:, 0, 1, :] = jnp.where(stays, own1_ref[0], other1_ref[0])


def place(m, stays, parts, so_far, deps):
    _, quarter, width = parts[0][0].shape
    specs = [pl.BlockSpec((1, quarter, width), functools.partial(lambda at, i: (at, 0, 0), at)) for _, at in parts]
    given = ([] if so_far is None else [so_far]) + list(deps)
    return pl.pallas_call(
        place_kernel,
        grid=(1,),
        in_specs=[pl.BlockSpec(memory_space=pltpu.SMEM)] + specs + [pl.BlockSpec(memory_space=pl.ANY)] * len(given),
        out_specs=pl.BlockSpec((quarter, 1, 2, width), lambda i: (0, m, 0, 0)),
        out_shape=jax.ShapeDtypeStruct((quarter, 3, 2, width), jnp.bfloat16),
        input_output_aliases={} if so_far is None else {5: 0},
        compiler_params=pltpu.CompilerParams(vmem_limit_bytes=VMEM),
        cost_estimate=pl.CostEstimate(flops=2 * quarter * width, bytes_accessed=12 * quarter * width, transcendentals=0),
        name="place",
    )(stays, *(array for array, _ in parts), *given)


GROUPS = (((0, 1, 2),), ((0,), (1,), (2,)))


def local(tokens, cotangent, router_probs, routes, partner, gate_weight, up_weight, down_weight):
    tok, width = tokens.shape
    owners = lax.axis_size("expert")
    slots = gate_weight.shape[0]
    routes_t, probs_t = routes.T, router_probs.T
    ids = (partner[None, :] * slots + jnp.arange(slots, dtype=jnp.int32)[:, None]).reshape(slots, owners, 1)
    here = lax.axis_index("expert")
    plane = lax.axis_index("dp").reshape(1)
    stays = (jnp.sum(jnp.where(jnp.arange(owners) == here, partner, 0)) == here).astype(jnp.int32).reshape(1)
    sends = dispatch(routes_t, probs_t, ids, tokens, cotangent, (plane, stays))
    backs, final, after_pair = [], {}, ()
    for slot in range(slots):
        groups = GROUPS[slot]
        recv = lax.all_to_all(sends[slot], "expert", split_axis=0, concat_axis=0, tiled=True)
        ahead, behind, hold, own, back = expert(
            slot, groups, plane, recv, gate_weight, up_weight, down_weight, after_pair
        )
        backs.append(lax.all_to_all(back, "expert", split_axis=0, concat_axis=0, tiled=True))
        from_behind = [shift(piece, "dp", 1) for piece in ahead]
        from_ahead = [shift(piece, "dp", -1) for piece in behind]
        totals = []
        for u, group in enumerate(groups):
            after = (totals[u - 2],) if u >= 2 else ()
            pair_a, pair_b = pair(hold[u], from_behind[u], from_ahead[u], after)
            if u == 0:
                after_pair = (pair_a, pair_b)
            pair_a, pair_b = shift(pair_a, "dp", 1), shift(pair_b, "dp", -1)
            total = finish(own[u], from_behind[u], from_ahead[u], pair_a, pair_b, ())
            totals.append(total)
            other = shift(total, "expert", owners // 2)
            for at, m in enumerate(group):
                final[slot, m] = [(total, at), (other, at)]
    output, token_grad = combine(routes_t, probs_t, (ids[0], ids[1]), backs, tok, width)
    grads = None
    for m in range(3):
        deps = (output,) if m == 2 else ()
        grads = place(m, stays, final[0, m] + final[1, m], grads, deps)
    return (output, token_grad, grads.transpose(0, 2, 1, 3))


def solution(mesh):
    rows = P(("expert", "dp"), None)
    by_slot = P("expert", None, None)
    return jax.shard_map(
        local,
        mesh=mesh,
        in_specs=(rows, rows, rows, rows, P(), by_slot, by_slot, by_slot),
        out_specs=(rows, rows, P("dp", "expert", None, None)),
        check_vma=False,
    )
```

```python
import functools
import jax
import jax.numpy as jnp
from jax import lax
from jax.experimental import pallas as pl
from jax.experimental.pallas import tpu as pltpu
from jax.sharding import PartitionSpec as P

CAP = 16
F_TILE = 256
D_TILE = 2048
SEND_ORDER = (4, 5, 3, 6, 2, 7, 0, 1)
VMEM = 58 * 1024 * 1024


def contract(a, b, dims):
    return lax.dot_general(a, b, (dims, ((), ())), preferred_element_type=jnp.float32)


def slot_matrix(routes_t, ids):
    owners = ids.shape[0]
    tok = routes_t.shape[1]
    hit = jnp.zeros((owners, tok), jnp.float32)
    for k in range(routes_t.shape[0]):
        hit = hit + (routes_t[k : k + 1, :] == ids).astype(jnp.float32)
    earlier = (
        lax.broadcasted_iota(jnp.int32, (tok, tok), 0) < lax.broadcasted_iota(jnp.int32, (tok, tok), 1)
    ).astype(jnp.bfloat16)
    rank = contract(hit.astype(jnp.bfloat16), earlier, ((1,), (0,)))
    rank = jnp.where(hit > 0.5, rank, -1.0)
    spread = jnp.broadcast_to(rank[:, None, :], (owners, CAP, tok)).reshape(owners * CAP, tok)
    place = (lax.broadcasted_iota(jnp.int32, (owners * CAP, tok), 0) % CAP).astype(jnp.float32)
    return spread == place


def slot_probs(routes_t, probs_t, ids, chosen):
    owners = ids.shape[0]
    tok = routes_t.shape[1]
    weight = jnp.zeros((owners, tok), jnp.float32)
    for k in range(routes_t.shape[0]):
        weight = weight + jnp.where(routes_t[k : k + 1, :] == ids, probs_t[k : k + 1, :], 0.0)
    spread = jnp.broadcast_to(weight[:, None, :], (owners, CAP, tok)).reshape(owners * CAP, tok)
    return jnp.where(chosen, spread, 0.0)


def dispatch_kernel(routes_ref, probs_ref, ids_ref, tokens_ref, cot_ref, *rest):
    slots, owners, _ = ids_ref.shape
    width = tokens_ref.shape[1]
    for slot, send_ref in enumerate(rest[len(rest) - slots :]):
        chosen = slot_matrix(routes_ref[...], ids_ref[slot])
        probs = slot_probs(routes_ref[...], probs_ref[...], ids_ref[slot], chosen)
        onehot = chosen.astype(jnp.bfloat16)
        row_prob = jnp.sum(probs, axis=1, keepdims=True)
        rows = contract(onehot, tokens_ref[...], ((1,), (0,))).astype(jnp.bfloat16)
        send_ref[:, 0] = rows.reshape(owners, CAP, width)
        cot = (row_prob * contract(onehot, cot_ref[...], ((1,), (0,)))).astype(jnp.bfloat16)
        send_ref[:, 1] = cot.reshape(owners, CAP, width)


def dispatch(routes_t, probs_t, ids, tokens, cotangent, deps):
    slots, owners, _ = ids.shape
    width = tokens.shape[1]
    vmem = pl.BlockSpec(memory_space=pltpu.VMEM)
    return pl.pallas_call(
        dispatch_kernel,
        in_specs=[vmem] * 5 + [pl.BlockSpec(memory_space=pl.ANY)] * len(deps),
        out_shape=[jax.ShapeDtypeStruct((owners, 2, CAP, width), jnp.bfloat16)] * slots,
        compiler_params=pltpu.CompilerParams(vmem_limit_bytes=VMEM),
        name="dispatch",
    )(routes_t, probs_t, ids, tokens, cotangent, *deps)


def expert_kernel(slot, units_of, deps, here_ref, recv_ref, gate_hbm, up_hbm, down_hbm, *rest):
    rest = rest[deps:]
    count = len(units_of)
    ahead, behind, hold, own, back_ref = (
        rest[:count],
        rest[count : 2 * count],
        rest[2 * count : 3 * count],
        rest[3 * count : 4 * count],
        rest[4 * count],
    )
    (gate_w, up_w, down_w, hidden, grad_pre, hidden_t, gate_t, up_t, grads, load_sem, save_sem) = rest[4 * count + 1 :]
    place_of = {m: (u, at) for u, group in enumerate(units_of) for at, m in enumerate(group)}
    owners, _, cap, width = recv_ref.shape
    units = gate_w.shape[1]
    n_rows = owners * cap
    here = here_ref[0]

    def load(i):
        cols = pl.ds(i * F_TILE, F_TILE)
        return (
            pltpu.make_async_copy(gate_hbm.at[slot, :, cols], gate_w.at[:, cols], load_sem.at[0, i]),
            pltpu.make_async_copy(up_hbm.at[slot, :, cols], up_w.at[:, cols], load_sem.at[1, i]),
            pltpu.make_async_copy(down_hbm.at[slot, cols], down_w.at[cols], load_sem.at[2, i]),
        )

    tiles = units // F_TILE
    for i in range(tiles):
        for copy in load(i):
            copy.start()
    rows = recv_ref[:, 0].reshape(n_rows, width)
    cot = recv_ref[:, 1].reshape(n_rows, width)
    for i in range(tiles):
        for copy in load(i):
            copy.wait()
        cols = pl.ds(i * F_TILE, F_TILE)
        gate_pre = contract(rows, gate_w[:, cols], ((1,), (0,)))
        up_proj = contract(rows, up_w[:, cols], ((1,), (0,)))
        grad_hidden = contract(cot, down_w[cols], ((1,), (1,)))
        sig = 1.0 / (1.0 + jnp.exp(-gate_pre))
        act = gate_pre * sig
        one_hidden = (act * up_proj).astype(jnp.bfloat16)
        one_gate = (grad_hidden * up_proj * sig * (1.0 + gate_pre * (1.0 - sig))).astype(jnp.bfloat16)
        one_up = (grad_hidden * act).astype(jnp.bfloat16)
        hidden[:, cols] = one_hidden
        grad_pre[0, :, cols] = one_gate
        grad_pre[1, :, cols] = one_up
        hidden_t[cols] = one_hidden.T
        gate_t[cols] = one_gate.T
        up_t[cols] = one_up.T

    quarter = units // 4
    half = quarter // 2

    def save(m, k):
        start = lax.rem(here + k // 2, 4) * quarter + (k % 2) * half
        source = grads.at[m, pl.ds(pl.multiple_of(start, 32), half), :]
        u, at = place_of[m]
        target = (
            own[u].at[at, pl.ds(0, half)],
            own[u].at[at, pl.ds(half, half)],
            hold[u].at[0, at],
            ahead[u].at[1, at],
            ahead[u].at[0, at],
            behind[u].at[0, at],
            behind[u].at[1, at],
            hold[u].at[1, at],
        )[k]
        return pltpu.make_async_copy(source, target, save_sem.at[m, k])

    for m, (left, second) in enumerate(((gate_t, 0), (up_t, 0), (hidden_t, 1))):

        def grad_chunk(j, carry, m=m, left=left, second=second):
            cols = pl.ds(pl.multiple_of(j * D_TILE, D_TILE), D_TILE)
            right = recv_ref[:, second, :, cols].reshape(n_rows, D_TILE)
            grads[m, :, cols] = contract(left[...], right, ((1,), (0,))).astype(jnp.bfloat16)
            return carry

        lax.fori_loop(0, width // D_TILE, grad_chunk, 0)
        for k in SEND_ORDER:
            save(m, k).start()

    def back_chunk(j, carry):
        cols = pl.ds(pl.multiple_of(j * D_TILE, D_TILE), D_TILE)
        out = contract(hidden[...], down_w[:, cols], ((1,), (0,)))
        back_ref[:, 0, :, cols] = out.astype(jnp.bfloat16).reshape(owners, cap, D_TILE)
        dx = contract(grad_pre[0], gate_w[cols], ((1,), (1,)))
        dx = dx + contract(grad_pre[1], up_w[cols], ((1,), (1,)))
        back_ref[:, 1, :, cols] = dx.astype(jnp.bfloat16).reshape(owners, cap, D_TILE)
        return carry

    lax.fori_loop(0, width // D_TILE, back_chunk, 0)
    for m in range(3):
        for k in SEND_ORDER:
            save(m, k).wait()


def expert(slot, units_of, here, recv, gate_weight, up_weight, down_weight, deps):
    owners, _, cap, width = recv.shape
    units = gate_weight.shape[2]
    rows = owners * cap
    half = units // 8
    anywhere = pl.BlockSpec(memory_space=pl.ANY)
    given = pl.BlockSpec((owners, 2, cap, width), lambda i: (0, 0, 0, 0))
    back = pl.BlockSpec((owners, 2, cap, width), lambda i: (0, 0, 0, 0))
    count = len(units_of)
    shapes = [(2, len(group), half, width) for group in units_of] * 3
    shapes += [(len(group), 2 * half, width) for group in units_of] + [(owners, 2, cap, width)]
    out = pl.pallas_call(
        functools.partial(expert_kernel, slot, units_of, len(deps)),
        grid=(1,),
        in_specs=[pl.BlockSpec(memory_space=pltpu.SMEM), given] + [anywhere] * (3 + len(deps)),
        out_specs=[anywhere] * (4 * count) + [back],
        out_shape=[jax.ShapeDtypeStruct(shape, jnp.bfloat16) for shape in shapes],
        scratch_shapes=[
            pltpu.VMEM((width, units), jnp.bfloat16),
            pltpu.VMEM((width, units), jnp.bfloat16),
            pltpu.VMEM((units, width), jnp.bfloat16),
            pltpu.VMEM((rows, units), jnp.bfloat16),
            pltpu.VMEM((2, rows, units), jnp.bfloat16),
            pltpu.VMEM((units, rows), jnp.bfloat16),
            pltpu.VMEM((units, rows), jnp.bfloat16),
            pltpu.VMEM((units, rows), jnp.bfloat16),
            pltpu.VMEM((3, units, width), jnp.bfloat16),
            pltpu.SemaphoreType.DMA((3, units // F_TILE)),
            pltpu.SemaphoreType.DMA((3, 8)),
        ],
        compiler_params=pltpu.CompilerParams(vmem_limit_bytes=VMEM),
        cost_estimate=pl.CostEstimate(
            flops=40 * rows * width * units,
            bytes_accessed=12 * width * units + 8 * rows * width,
            transcendentals=rows * units,
        ),
        name="expert",
    )(here, recv, gate_weight, up_weight, down_weight, *deps)
    return tuple(out[i * count : (i + 1) * count] for i in range(4)) + (out[4 * count],)


def combine_kernel(routes_ref, probs_ref, ids0_ref, ids1_ref, back0_ref, back1_ref, output_ref, grad_ref):
    width = output_ref.shape[1]
    output, grad = None, None
    for ids_ref, back_ref in ((ids0_ref, back0_ref), (ids1_ref, back1_ref)):
        rows = ids_ref.shape[0] * CAP
        chosen = slot_matrix(routes_ref[...], ids_ref[...])
        probs = slot_probs(routes_ref[...], probs_ref[...], ids_ref[...], chosen)
        high = probs.astype(jnp.bfloat16)
        low = (probs - high.astype(jnp.float32)).astype(jnp.bfloat16)
        out_rows = back_ref[:, 0].reshape(rows, width)
        dx_rows = back_ref[:, 1].reshape(rows, width)
        one_out = contract(high, out_rows, ((0,), (0,))) + contract(low, out_rows, ((0,), (0,)))
        one_grad = contract(chosen.astype(jnp.bfloat16), dx_rows, ((0,), (0,)))
        output = one_out if output is None else output + one_out
        grad = one_grad if grad is None else grad + one_grad
    output_ref[...] = output.astype(jnp.bfloat16)
    grad_ref[...] = grad.astype(jnp.bfloat16)


def combine(routes_t, probs_t, ids, backs, tok, width):
    row = jax.ShapeDtypeStruct((tok, width), jnp.bfloat16)
    return pl.pallas_call(
        combine_kernel,
        out_shape=[row, row],
        compiler_params=pltpu.CompilerParams(vmem_limit_bytes=VMEM),
        name="combine",
    )(routes_t, probs_t, *ids, *backs)


def shift(value, axis, by):
    n = lax.axis_size(axis)
    return lax.ppermute(value, axis, [(i, (i + by) % n) for i in range(n)])


def add(*terms):
    total = terms[0].astype(jnp.float32)
    for term in terms[1:]:
        total = total + term.astype(jnp.float32)
    return total.astype(jnp.bfloat16)


def spread_call(kernel, name, count, inputs, out_shapes, deps):
    specs = []
    for array, at in inputs:
        rows, width = array.shape[-2:]
        if at is None:
            specs.append(pl.BlockSpec((1, rows, width), lambda i: (i, 0, 0)))
        else:
            specs.append(pl.BlockSpec((1, 1, rows, width), functools.partial(lambda at, i: (at, i, 0, 0), at)))
    size = sum(shape[0] * shape[1] for shape in out_shapes)
    return pl.pallas_call(
        kernel,
        grid=(count,),
        in_specs=specs + [pl.BlockSpec(memory_space=pl.ANY)] * len(deps),
        out_specs=[pl.BlockSpec((1, *shape), lambda i: (i, 0, 0)) for shape in out_shapes],
        out_shape=[jax.ShapeDtypeStruct((count, *shape), jnp.bfloat16) for shape in out_shapes],
        compiler_params=pltpu.CompilerParams(vmem_limit_bytes=VMEM),
        cost_estimate=pl.CostEstimate(flops=2 * count * size, bytes_accessed=6 * count * size, transcendentals=0),
        name=name,
    )(*(array for array, _ in inputs), *deps)


def pair_kernel(hold_a_ref, hold_b_ref, far_a_ref, far_b_ref, *rest):
    pair_a_ref, pair_b_ref = rest[-2:]
    pair_a_ref[0] = add(hold_a_ref[0, 0], far_a_ref[0, 0])
    pair_b_ref[0] = add(hold_b_ref[0, 0], far_b_ref[0, 0])


def pair(hold, from_behind, from_ahead, deps):
    _, count, half, width = hold.shape
    inputs = [(hold, 0), (hold, 1), (from_behind, 0), (from_ahead, 0)]
    return spread_call(pair_kernel, "pair", count, inputs, [(half, width)] * 2, deps)


def finish_kernel(own_ref, near_a_ref, near_b_ref, pair_a_ref, pair_b_ref, *rest):
    sum_ref = rest[-1]
    half = pair_a_ref.shape[1]
    sum_ref[0, :half] = add(own_ref[0, :half], near_a_ref[0, 0], pair_a_ref[0])
    sum_ref[0, half:] = add(own_ref[0, half:], near_b_ref[0, 0], pair_b_ref[0])


def finish(own, from_behind, from_ahead, pair_a, pair_b, first, count):
    _, quarter, width = own.shape
    half = quarter // 2

    def near(i):
        return (1, first + i, 0, 0)

    def at(i):
        return (first + i, 0, 0)

    return pl.pallas_call(
        finish_kernel,
        grid=(count,),
        in_specs=[
            pl.BlockSpec((1, quarter, width), at),
            pl.BlockSpec((1, 1, half, width), near),
            pl.BlockSpec((1, 1, half, width), near),
            pl.BlockSpec((1, half, width), at),
            pl.BlockSpec((1, half, width), at),
        ],
        out_specs=pl.BlockSpec((1, quarter, width), lambda i: (i, 0, 0)),
        out_shape=jax.ShapeDtypeStruct((count, quarter, width), jnp.bfloat16),
        compiler_params=pltpu.CompilerParams(vmem_limit_bytes=VMEM),
        cost_estimate=pl.CostEstimate(
            flops=3 * count * quarter * width, bytes_accessed=8 * count * quarter * width, transcendentals=0
        ),
        name="finish",
    )(own, from_ahead, from_behind, pair_a, pair_b)


def place_kernel(stays_ref, own0_ref, other0_ref, own1_ref, other1_ref, *rest):
    out_ref = rest[-1]
    stays = stays_ref[0] == 1
    out_ref[:, 0, 0, :] = jnp.where(stays, own0_ref[0], other0_ref[0])
    out_ref[:, 0, 1, :] = jnp.where(stays, own1_ref[0], other1_ref[0])


def place(m, stays, parts, so_far, deps):
    _, quarter, width = parts[0][0].shape
    specs = [pl.BlockSpec((1, quarter, width), functools.partial(lambda at, i: (at, 0, 0), at)) for _, at in parts]
    given = ([] if so_far is None else [so_far]) + list(deps)
    return pl.pallas_call(
        place_kernel,
        grid=(1,),
        in_specs=[pl.BlockSpec(memory_space=pltpu.SMEM)] + specs + [pl.BlockSpec(memory_space=pl.ANY)] * len(given),
        out_specs=pl.BlockSpec((quarter, 1, 2, width), lambda i: (0, m, 0, 0)),
        out_shape=jax.ShapeDtypeStruct((quarter, 3, 2, width), jnp.bfloat16),
        input_output_aliases={} if so_far is None else {5: 0},
        compiler_params=pltpu.CompilerParams(vmem_limit_bytes=VMEM),
        cost_estimate=pl.CostEstimate(flops=2 * quarter * width, bytes_accessed=12 * quarter * width, transcendentals=0),
        name="place",
    )(stays, *(array for array, _ in parts), *given)


GROUPS = (((0, 1, 2),), ((0,), (1, 2)))


def local(tokens, cotangent, router_probs, routes, partner, gate_weight, up_weight, down_weight):
    tok, width = tokens.shape
    owners = lax.axis_size("expert")
    slots = gate_weight.shape[0]
    routes_t, probs_t = routes.T, router_probs.T
    ids = (partner[None, :] * slots + jnp.arange(slots, dtype=jnp.int32)[:, None]).reshape(slots, owners, 1)
    here = lax.axis_index("expert")
    plane = lax.axis_index("dp").reshape(1)
    stays = (jnp.sum(jnp.where(jnp.arange(owners) == here, partner, 0)) == here).astype(jnp.int32).reshape(1)
    sends = dispatch(routes_t, probs_t, ids, tokens, cotangent, (plane, stays))
    backs, final, after_pair = [], {}, ()
    for slot in range(slots):
        groups = GROUPS[slot]
        recv = lax.all_to_all(sends[slot], "expert", split_axis=0, concat_axis=0, tiled=True)
        ahead, behind, hold, own, back = expert(
            slot, groups, plane, recv, gate_weight, up_weight, down_weight, after_pair
        )
        backs.append(lax.all_to_all(back, "expert", split_axis=0, concat_axis=0, tiled=True))
        from_behind = [shift(piece, "dp", 1) for piece in ahead]
        from_ahead = [shift(piece, "dp", -1) for piece in behind]
        totals = []
        for u, group in enumerate(groups):
            pair_a, pair_b = pair(hold[u], from_behind[u], from_ahead[u], tuple(totals))
            if u == 0:
                after_pair = (pair_a, pair_b)
            pair_a, pair_b = shift(pair_a, "dp", 1), shift(pair_b, "dp", -1)
            at_once = len(group) if slot == 0 else 1
            for first in range(0, len(group), at_once):
                total = finish(own[u], from_behind[u], from_ahead[u], pair_a, pair_b, first, at_once)
                totals.append(total)
                other = shift(total, "expert", owners // 2)
                for at in range(at_once):
                    final[slot, group[first + at]] = [(total, at), (other, at)]
    output, token_grad = combine(routes_t, probs_t, (ids[0], ids[1]), backs, tok, width)
    grads = None
    for m in range(3):
        deps = (output,) if m == 2 else ()
        grads = place(m, stays, final[0, m] + final[1, m], grads, deps)
    return (output, token_grad, grads.transpose(0, 2, 1, 3))


def solution(mesh):
    rows = P(("expert", "dp"), None)
    by_slot = P("expert", None, None)
    return jax.shard_map(
        local,
        mesh=mesh,
        in_specs=(rows, rows, rows, rows, P(), by_slot, by_slot, by_slot),
        out_specs=(rows, rows, P("dp", "expert", None, None)),
        check_vma=False,
    )
```

```python
import functools
import jax
import jax.numpy as jnp
from jax import lax
from jax.experimental import pallas as pl
from jax.experimental.pallas import tpu as pltpu
from jax.sharding import PartitionSpec as P

CAP = 16
F_TILE = 256
D_TILE = 2048
SEND_ORDER = (4, 5, 3, 6, 2, 7, 0, 1)
VMEM = 58 * 1024 * 1024


def contract(a, b, dims):
    return lax.dot_general(a, b, (dims, ((), ())), preferred_element_type=jnp.float32)


def slot_matrix(routes_t, ids):
    owners = ids.shape[0]
    tok = routes_t.shape[1]
    hit = jnp.zeros((owners, tok), jnp.float32)
    for k in range(routes_t.shape[0]):
        hit = hit + (routes_t[k : k + 1, :] == ids).astype(jnp.float32)
    earlier = (
        lax.broadcasted_iota(jnp.int32, (tok, tok), 0) < lax.broadcasted_iota(jnp.int32, (tok, tok), 1)
    ).astype(jnp.bfloat16)
    rank = contract(hit.astype(jnp.bfloat16), earlier, ((1,), (0,)))
    rank = jnp.where(hit > 0.5, rank, -1.0)
    spread = jnp.broadcast_to(rank[:, None, :], (owners, CAP, tok)).reshape(owners * CAP, tok)
    place = (lax.broadcasted_iota(jnp.int32, (owners * CAP, tok), 0) % CAP).astype(jnp.float32)
    return spread == place


def slot_probs(routes_t, probs_t, ids, chosen):
    owners = ids.shape[0]
    tok = routes_t.shape[1]
    weight = jnp.zeros((owners, tok), jnp.float32)
    for k in range(routes_t.shape[0]):
        weight = weight + jnp.where(routes_t[k : k + 1, :] == ids, probs_t[k : k + 1, :], 0.0)
    spread = jnp.broadcast_to(weight[:, None, :], (owners, CAP, tok)).reshape(owners * CAP, tok)
    return jnp.where(chosen, spread, 0.0)


def dispatch_kernel(routes_ref, probs_ref, ids_ref, tokens_ref, cot_ref, *rest):
    slots, owners, _ = ids_ref.shape
    width = tokens_ref.shape[1]
    for slot, send_ref in enumerate(rest[len(rest) - slots :]):
        chosen = slot_matrix(routes_ref[...], ids_ref[slot])
        probs = slot_probs(routes_ref[...], probs_ref[...], ids_ref[slot], chosen)
        onehot = chosen.astype(jnp.bfloat16)
        row_prob = jnp.sum(probs, axis=1, keepdims=True)
        rows = contract(onehot, tokens_ref[...], ((1,), (0,))).astype(jnp.bfloat16)
        send_ref[:, 0] = rows.reshape(owners, CAP, width)
        cot = (row_prob * contract(onehot, cot_ref[...], ((1,), (0,)))).astype(jnp.bfloat16)
        send_ref[:, 1] = cot.reshape(owners, CAP, width)


def dispatch(routes_t, probs_t, ids, tokens, cotangent, deps):
    slots, owners, _ = ids.shape
    width = tokens.shape[1]
    vmem = pl.BlockSpec(memory_space=pltpu.VMEM)
    return pl.pallas_call(
        dispatch_kernel,
        in_specs=[vmem] * 5 + [pl.BlockSpec(memory_space=pl.ANY)] * len(deps),
        out_shape=[jax.ShapeDtypeStruct((owners, 2, CAP, width), jnp.bfloat16)] * slots,
        compiler_params=pltpu.CompilerParams(vmem_limit_bytes=VMEM),
        name="dispatch",
    )(routes_t, probs_t, ids, tokens, cotangent, *deps)


def expert_kernel(slot, units_of, deps, here_ref, recv_ref, gate_hbm, up_hbm, down_hbm, *rest):
    rest = rest[deps:]
    count = len(units_of)
    ahead, behind, hold, own, back_ref = (
        rest[:count],
        rest[count : 2 * count],
        rest[2 * count : 3 * count],
        rest[3 * count : 4 * count],
        rest[4 * count],
    )
    (gate_w, up_w, down_w, hidden, grad_pre, hidden_t, gate_t, up_t, grads, load_sem, save_sem) = rest[4 * count + 1 :]
    place_of = {m: (u, at) for u, group in enumerate(units_of) for at, m in enumerate(group)}
    owners, _, cap, width = recv_ref.shape
    units = gate_w.shape[1]
    n_rows = owners * cap
    here = here_ref[0]

    def load(i):
        cols = pl.ds(i * F_TILE, F_TILE)
        return (
            pltpu.make_async_copy(gate_hbm.at[slot, :, cols], gate_w.at[:, cols], load_sem.at[0, i]),
            pltpu.make_async_copy(up_hbm.at[slot, :, cols], up_w.at[:, cols], load_sem.at[1, i]),
            pltpu.make_async_copy(down_hbm.at[slot, cols], down_w.at[cols], load_sem.at[2, i]),
        )

    tiles = units // F_TILE
    for i in range(tiles):
        for copy in load(i):
            copy.start()
    rows = recv_ref[:, 0].reshape(n_rows, width)
    cot = recv_ref[:, 1].reshape(n_rows, width)
    for i in range(tiles):
        for copy in load(i):
            copy.wait()
        cols = pl.ds(i * F_TILE, F_TILE)
        gate_pre = contract(rows, gate_w[:, cols], ((1,), (0,)))
        up_proj = contract(rows, up_w[:, cols], ((1,), (0,)))
        grad_hidden = contract(cot, down_w[cols], ((1,), (1,)))
        sig = 1.0 / (1.0 + jnp.exp(-gate_pre))
        act = gate_pre * sig
        one_hidden = (act * up_proj).astype(jnp.bfloat16)
        one_gate = (grad_hidden * up_proj * sig * (1.0 + gate_pre * (1.0 - sig))).astype(jnp.bfloat16)
        one_up = (grad_hidden * act).astype(jnp.bfloat16)
        hidden[:, cols] = one_hidden
        grad_pre[0, :, cols] = one_gate
        grad_pre[1, :, cols] = one_up
        hidden_t[cols] = one_hidden.T
        gate_t[cols] = one_gate.T
        up_t[cols] = one_up.T

    quarter = units // 4
    half = quarter // 2

    def save(m, k):
        start = lax.rem(here + k // 2, 4) * quarter + (k % 2) * half
        source = grads.at[m, pl.ds(pl.multiple_of(start, 32), half), :]
        u, at = place_of[m]
        target = (
            own[u].at[at, pl.ds(0, half)],
            own[u].at[at, pl.ds(half, half)],
            hold[u].at[0, at],
            ahead[u].at[1, at],
            ahead[u].at[0, at],
            behind[u].at[0, at],
            behind[u].at[1, at],
            hold[u].at[1, at],
        )[k]
        return pltpu.make_async_copy(source, target, save_sem.at[m, k])

    for m, (left, second) in enumerate(((gate_t, 0), (up_t, 0), (hidden_t, 1))):

        def grad_chunk(j, carry, m=m, left=left, second=second):
            cols = pl.ds(pl.multiple_of(j * D_TILE, D_TILE), D_TILE)
            right = recv_ref[:, second, :, cols].reshape(n_rows, D_TILE)
            grads[m, :, cols] = contract(left[...], right, ((1,), (0,))).astype(jnp.bfloat16)
            return carry

        lax.fori_loop(0, width // D_TILE, grad_chunk, 0)
        for k in SEND_ORDER:
            save(m, k).start()

    def back_chunk(j, carry):
        cols = pl.ds(pl.multiple_of(j * D_TILE, D_TILE), D_TILE)
        out = contract(hidden[...], down_w[:, cols], ((1,), (0,)))
        back_ref[:, 0, :, cols] = out.astype(jnp.bfloat16).reshape(owners, cap, D_TILE)
        dx = contract(grad_pre[0], gate_w[cols], ((1,), (1,)))
        dx = dx + contract(grad_pre[1], up_w[cols], ((1,), (1,)))
        back_ref[:, 1, :, cols] = dx.astype(jnp.bfloat16).reshape(owners, cap, D_TILE)
        return carry

    lax.fori_loop(0, width // D_TILE, back_chunk, 0)
    for m in range(3):
        for k in SEND_ORDER:
            save(m, k).wait()


def expert(slot, units_of, here, recv, gate_weight, up_weight, down_weight, deps):
    owners, _, cap, width = recv.shape
    units = gate_weight.shape[2]
    rows = owners * cap
    half = units // 8
    anywhere = pl.BlockSpec(memory_space=pl.ANY)
    given = pl.BlockSpec((owners, 2, cap, width), lambda i: (0, 0, 0, 0))
    back = pl.BlockSpec((owners, 2, cap, width), lambda i: (0, 0, 0, 0))
    count = len(units_of)
    shapes = [(2, len(group), half, width) for group in units_of] * 3
    shapes += [(len(group), 2 * half, width) for group in units_of] + [(owners, 2, cap, width)]
    out = pl.pallas_call(
        functools.partial(expert_kernel, slot, units_of, len(deps)),
        grid=(1,),
        in_specs=[pl.BlockSpec(memory_space=pltpu.SMEM), given] + [anywhere] * (3 + len(deps)),
        out_specs=[anywhere] * (4 * count) + [back],
        out_shape=[jax.ShapeDtypeStruct(shape, jnp.bfloat16) for shape in shapes],
        scratch_shapes=[
            pltpu.VMEM((width, units), jnp.bfloat16),
            pltpu.VMEM((width, units), jnp.bfloat16),
            pltpu.VMEM((units, width), jnp.bfloat16),
            pltpu.VMEM((rows, units), jnp.bfloat16),
            pltpu.VMEM((2, rows, units), jnp.bfloat16),
            pltpu.VMEM((units, rows), jnp.bfloat16),
            pltpu.VMEM((units, rows), jnp.bfloat16),
            pltpu.VMEM((units, rows), jnp.bfloat16),
            pltpu.VMEM((3, units, width), jnp.bfloat16),
            pltpu.SemaphoreType.DMA((3, units // F_TILE)),
            pltpu.SemaphoreType.DMA((3, 8)),
        ],
        compiler_params=pltpu.CompilerParams(vmem_limit_bytes=VMEM),
        cost_estimate=pl.CostEstimate(
            flops=40 * rows * width * units,
            bytes_accessed=12 * width * units + 8 * rows * width,
            transcendentals=rows * units,
        ),
        name="expert",
    )(here, recv, gate_weight, up_weight, down_weight, *deps)
    return tuple(out[i * count : (i + 1) * count] for i in range(4)) + (out[4 * count],)


def combine_kernel(routes_ref, probs_ref, ids0_ref, ids1_ref, back0_ref, back1_ref, output_ref, grad_ref):
    width = output_ref.shape[1]
    output, grad = None, None
    for ids_ref, back_ref in ((ids0_ref, back0_ref), (ids1_ref, back1_ref)):
        rows = ids_ref.shape[0] * CAP
        chosen = slot_matrix(routes_ref[...], ids_ref[...])
        probs = slot_probs(routes_ref[...], probs_ref[...], ids_ref[...], chosen)
        high = probs.astype(jnp.bfloat16)
        low = (probs - high.astype(jnp.float32)).astype(jnp.bfloat16)
        out_rows = back_ref[:, 0].reshape(rows, width)
        dx_rows = back_ref[:, 1].reshape(rows, width)
        one_out = contract(high, out_rows, ((0,), (0,))) + contract(low, out_rows, ((0,), (0,)))
        one_grad = contract(chosen.astype(jnp.bfloat16), dx_rows, ((0,), (0,)))
        output = one_out if output is None else output + one_out
        grad = one_grad if grad is None else grad + one_grad
    output_ref[...] = output.astype(jnp.bfloat16)
    grad_ref[...] = grad.astype(jnp.bfloat16)


def combine(routes_t, probs_t, ids, backs, tok, width):
    row = jax.ShapeDtypeStruct((tok, width), jnp.bfloat16)
    return pl.pallas_call(
        combine_kernel,
        out_shape=[row, row],
        compiler_params=pltpu.CompilerParams(vmem_limit_bytes=VMEM),
        name="combine",
    )(routes_t, probs_t, *ids, *backs)


def shift(value, axis, by):
    n = lax.axis_size(axis)
    return lax.ppermute(value, axis, [(i, (i + by) % n) for i in range(n)])


def add(*terms):
    total = terms[0].astype(jnp.float32)
    for term in terms[1:]:
        total = total + term.astype(jnp.float32)
    return total.astype(jnp.bfloat16)


def spread_call(kernel, name, count, inputs, out_shapes, deps):
    specs = []
    for array, at in inputs:
        rows, width = array.shape[-2:]
        if at is None:
            specs.append(pl.BlockSpec((1, rows, width), lambda i: (i, 0, 0)))
        else:
            specs.append(pl.BlockSpec((1, 1, rows, width), functools.partial(lambda at, i: (at, i, 0, 0), at)))
    size = sum(shape[0] * shape[1] for shape in out_shapes)
    return pl.pallas_call(
        kernel,
        grid=(count,),
        in_specs=specs + [pl.BlockSpec(memory_space=pl.ANY)] * len(deps),
        out_specs=[pl.BlockSpec((1, *shape), lambda i: (i, 0, 0)) for shape in out_shapes],
        out_shape=[jax.ShapeDtypeStruct((count, *shape), jnp.bfloat16) for shape in out_shapes],
        compiler_params=pltpu.CompilerParams(vmem_limit_bytes=VMEM),
        cost_estimate=pl.CostEstimate(flops=2 * count * size, bytes_accessed=6 * count * size, transcendentals=0),
        name=name,
    )(*(array for array, _ in inputs), *deps)


def pair_kernel(hold_a_ref, hold_b_ref, far_a_ref, far_b_ref, *rest):
    pair_a_ref, pair_b_ref = rest[-2:]
    pair_a_ref[0] = add(hold_a_ref[0, 0], far_a_ref[0, 0])
    pair_b_ref[0] = add(hold_b_ref[0, 0], far_b_ref[0, 0])


def pair(hold, from_behind, from_ahead, deps):
    _, count, half, width = hold.shape
    inputs = [(hold, 0), (hold, 1), (from_behind, 0), (from_ahead, 0)]
    return spread_call(pair_kernel, "pair", count, inputs, [(half, width)] * 2, deps)


def finish_kernel(own_ref, near_a_ref, near_b_ref, pair_a_ref, pair_b_ref, *rest):
    sum_ref = rest[-1]
    half = pair_a_ref.shape[1]
    sum_ref[0, :half] = add(own_ref[0, :half], near_a_ref[0, 0], pair_a_ref[0])
    sum_ref[0, half:] = add(own_ref[0, half:], near_b_ref[0, 0], pair_b_ref[0])


def finish(own, from_behind, from_ahead, pair_a, pair_b, first, count, deps):
    _, quarter, width = own.shape
    half = quarter // 2

    def near(i):
        return (1, first + i, 0, 0)

    def at(i):
        return (first + i, 0, 0)

    return pl.pallas_call(
        finish_kernel,
        grid=(count,),
        in_specs=[
            pl.BlockSpec((1, quarter, width), at),
            pl.BlockSpec((1, 1, half, width), near),
            pl.BlockSpec((1, 1, half, width), near),
            pl.BlockSpec((1, half, width), at),
            pl.BlockSpec((1, half, width), at),
        ]
        + [pl.BlockSpec(memory_space=pl.ANY)] * len(deps),
        out_specs=pl.BlockSpec((1, quarter, width), lambda i: (i, 0, 0)),
        out_shape=jax.ShapeDtypeStruct((count, quarter, width), jnp.bfloat16),
        compiler_params=pltpu.CompilerParams(vmem_limit_bytes=VMEM),
        cost_estimate=pl.CostEstimate(
            flops=3 * count * quarter * width, bytes_accessed=8 * count * quarter * width, transcendentals=0
        ),
        name="finish",
    )(own, from_ahead, from_behind, pair_a, pair_b, *deps)


def place_kernel(stays_ref, own0_ref, other0_ref, own1_ref, other1_ref, *rest):
    out_ref = rest[-1]
    stays = stays_ref[0] == 1
    out_ref[:, 0, 0, :] = jnp.where(stays, own0_ref[0], other0_ref[0])
    out_ref[:, 0, 1, :] = jnp.where(stays, own1_ref[0], other1_ref[0])


def place(m, stays, parts, so_far, deps):
    _, quarter, width = parts[0][0].shape
    specs = [pl.BlockSpec((1, quarter, width), functools.partial(lambda at, i: (at, 0, 0), at)) for _, at in parts]
    given = ([] if so_far is None else [so_far]) + list(deps)
    return pl.pallas_call(
        place_kernel,
        grid=(1,),
        in_specs=[pl.BlockSpec(memory_space=pltpu.SMEM)] + specs + [pl.BlockSpec(memory_space=pl.ANY)] * len(given),
        out_specs=pl.BlockSpec((quarter, 1, 2, width), lambda i: (0, m, 0, 0)),
        out_shape=jax.ShapeDtypeStruct((quarter, 3, 2, width), jnp.bfloat16),
        input_output_aliases={} if so_far is None else {5: 0},
        compiler_params=pltpu.CompilerParams(vmem_limit_bytes=VMEM),
        cost_estimate=pl.CostEstimate(flops=2 * quarter * width, bytes_accessed=12 * quarter * width, transcendentals=0),
        name="place",
    )(stays, *(array for array, _ in parts), *given)


GROUPS = (((0, 1, 2),), ((1, 2), (0,)))


def local(tokens, cotangent, router_probs, routes, partner, gate_weight, up_weight, down_weight):
    tok, width = tokens.shape
    owners = lax.axis_size("expert")
    slots = gate_weight.shape[0]
    routes_t, probs_t = routes.T, router_probs.T
    ids = (partner[None, :] * slots + jnp.arange(slots, dtype=jnp.int32)[:, None]).reshape(slots, owners, 1)
    here = lax.axis_index("expert")
    plane = lax.axis_index("dp").reshape(1)
    stays = (jnp.sum(jnp.where(jnp.arange(owners) == here, partner, 0)) == here).astype(jnp.int32).reshape(1)
    sends = dispatch(routes_t, probs_t, ids, tokens, cotangent, (plane, stays))
    backs, final, after_pair = [], {}, ()
    for slot in range(slots):
        groups = GROUPS[slot]
        recv = lax.all_to_all(sends[slot], "expert", split_axis=0, concat_axis=0, tiled=True)
        ahead, behind, hold, own, back = expert(
            slot, groups, plane, recv, gate_weight, up_weight, down_weight, after_pair
        )
        backs.append(lax.all_to_all(back, "expert", split_axis=0, concat_axis=0, tiled=True))
        from_behind = [shift(piece, "dp", 1) for piece in ahead]
        from_ahead = [shift(piece, "dp", -1) for piece in behind]
        totals = []
        for u, group in enumerate(groups):
            pair_a, pair_b = pair(hold[u], from_behind[u], from_ahead[u], ())
            if u == 0:
                after_pair = (pair_a, pair_b)
            pair_a, pair_b = shift(pair_a, "dp", 1), shift(pair_b, "dp", -1)
            at_once = len(group) if slot == 0 else 1
            deps = tuple(totals)
            for first in range(0, len(group), at_once):
                total = finish(own[u], from_behind[u], from_ahead[u], pair_a, pair_b, first, at_once, deps)
                totals.append(total)
                other = shift(total, "expert", owners // 2)
                for at in range(at_once):
                    final[slot, group[first + at]] = [(total, at), (other, at)]
    output, token_grad = combine(routes_t, probs_t, (ids[0], ids[1]), backs, tok, width)
    grads = None
    for m in (1, 2, 0):
        deps = (output,) if m == 0 else ()
        grads = place(m, stays, final[0, m] + final[1, m], grads, deps)
    return (output, token_grad, grads.transpose(0, 2, 1, 3))


def solution(mesh):
    rows = P(("expert", "dp"), None)
    by_slot = P("expert", None, None)
    return jax.shard_map(
        local,
        mesh=mesh,
        in_specs=(rows, rows, rows, rows, P(), by_slot, by_slot, by_slot),
        out_specs=(rows, rows, P("dp", "expert", None, None)),
        check_vma=False,
    )
```

```python
import functools
import jax
import jax.numpy as jnp
from jax import lax
from jax.experimental import pallas as pl
from jax.experimental.pallas import tpu as pltpu
from jax.sharding import PartitionSpec as P

CAP = 16
F_TILE = 256
D_TILE = 2048
SEND_ORDER = (4, 5, 3, 6, 2, 7, 0, 1)
VMEM = 58 * 1024 * 1024


def contract(a, b, dims):
    return lax.dot_general(a, b, (dims, ((), ())), preferred_element_type=jnp.float32)


def slot_matrix(routes_t, ids):
    owners = ids.shape[0]
    tok = routes_t.shape[1]
    hit = jnp.zeros((owners, tok), jnp.float32)
    for k in range(routes_t.shape[0]):
        hit = hit + (routes_t[k : k + 1, :] == ids).astype(jnp.float32)
    earlier = (
        lax.broadcasted_iota(jnp.int32, (tok, tok), 0) < lax.broadcasted_iota(jnp.int32, (tok, tok), 1)
    ).astype(jnp.bfloat16)
    rank = contract(hit.astype(jnp.bfloat16), earlier, ((1,), (0,)))
    rank = jnp.where(hit > 0.5, rank, -1.0)
    spread = jnp.broadcast_to(rank[:, None, :], (owners, CAP, tok)).reshape(owners * CAP, tok)
    place = (lax.broadcasted_iota(jnp.int32, (owners * CAP, tok), 0) % CAP).astype(jnp.float32)
    return spread == place


def slot_probs(routes_t, probs_t, ids, chosen):
    owners = ids.shape[0]
    tok = routes_t.shape[1]
    weight = jnp.zeros((owners, tok), jnp.float32)
    for k in range(routes_t.shape[0]):
        weight = weight + jnp.where(routes_t[k : k + 1, :] == ids, probs_t[k : k + 1, :], 0.0)
    spread = jnp.broadcast_to(weight[:, None, :], (owners, CAP, tok)).reshape(owners * CAP, tok)
    return jnp.where(chosen, spread, 0.0)


def dispatch_kernel(routes_ref, probs_ref, ids_ref, tokens_ref, cot_ref, *rest):
    slots, owners, _ = ids_ref.shape
    width = tokens_ref.shape[1]
    for slot, send_ref in enumerate(rest[len(rest) - slots :]):
        chosen = slot_matrix(routes_ref[...], ids_ref[slot])
        probs = slot_probs(routes_ref[...], probs_ref[...], ids_ref[slot], chosen)
        onehot = chosen.astype(jnp.bfloat16)
        row_prob = jnp.sum(probs, axis=1, keepdims=True)
        rows = contract(onehot, tokens_ref[...], ((1,), (0,))).astype(jnp.bfloat16)
        send_ref[:, 0] = rows.reshape(owners, CAP, width)
        cot = (row_prob * contract(onehot, cot_ref[...], ((1,), (0,)))).astype(jnp.bfloat16)
        send_ref[:, 1] = cot.reshape(owners, CAP, width)


def dispatch(routes_t, probs_t, ids, tokens, cotangent, deps):
    slots, owners, _ = ids.shape
    width = tokens.shape[1]
    vmem = pl.BlockSpec(memory_space=pltpu.VMEM)
    return pl.pallas_call(
        dispatch_kernel,
        in_specs=[vmem] * 5 + [pl.BlockSpec(memory_space=pl.ANY)] * len(deps),
        out_shape=[jax.ShapeDtypeStruct((owners, 2, CAP, width), jnp.bfloat16)] * slots,
        compiler_params=pltpu.CompilerParams(vmem_limit_bytes=VMEM),
        name="dispatch",
    )(routes_t, probs_t, ids, tokens, cotangent, *deps)


def expert_kernel(slot, units_of, deps, here_ref, recv_ref, gate_hbm, up_hbm, down_hbm, *rest):
    rest = rest[deps:]
    count = len(units_of)
    ahead, behind, hold, own, back_ref = (
        rest[:count],
        rest[count : 2 * count],
        rest[2 * count : 3 * count],
        rest[3 * count : 4 * count],
        rest[4 * count],
    )
    (gate_w, up_w, down_w, hidden, grad_pre, hidden_t, gate_t, up_t, grads, load_sem, save_sem) = rest[4 * count + 1 :]
    place_of = {m: (u, at) for u, group in enumerate(units_of) for at, m in enumerate(group)}
    owners, _, cap, width = recv_ref.shape
    units = gate_w.shape[1]
    n_rows = owners * cap
    here = here_ref[0]

    def load(i):
        cols = pl.ds(i * F_TILE, F_TILE)
        return (
            pltpu.make_async_copy(gate_hbm.at[slot, :, cols], gate_w.at[:, cols], load_sem.at[0, i]),
            pltpu.make_async_copy(up_hbm.at[slot, :, cols], up_w.at[:, cols], load_sem.at[1, i]),
            pltpu.make_async_copy(down_hbm.at[slot, cols], down_w.at[cols], load_sem.at[2, i]),
        )

    tiles = units // F_TILE
    for i in range(tiles):
        for copy in load(i):
            copy.start()
    rows = recv_ref[:, 0].reshape(n_rows, width)
    cot = recv_ref[:, 1].reshape(n_rows, width)
    for i in range(tiles):
        for copy in load(i):
            copy.wait()
        cols = pl.ds(i * F_TILE, F_TILE)
        gate_pre = contract(rows, gate_w[:, cols], ((1,), (0,)))
        up_proj = contract(rows, up_w[:, cols], ((1,), (0,)))
        grad_hidden = contract(cot, down_w[cols], ((1,), (1,)))
        sig = 1.0 / (1.0 + jnp.exp(-gate_pre))
        act = gate_pre * sig
        one_hidden = (act * up_proj).astype(jnp.bfloat16)
        one_gate = (grad_hidden * up_proj * sig * (1.0 + gate_pre * (1.0 - sig))).astype(jnp.bfloat16)
        one_up = (grad_hidden * act).astype(jnp.bfloat16)
        hidden[:, cols] = one_hidden
        grad_pre[0, :, cols] = one_gate
        grad_pre[1, :, cols] = one_up
        hidden_t[cols] = one_hidden.T
        gate_t[cols] = one_gate.T
        up_t[cols] = one_up.T

    quarter = units // 4
    half = quarter // 2

    def save(m, k):
        start = lax.rem(here + k // 2, 4) * quarter + (k % 2) * half
        source = grads.at[m, pl.ds(pl.multiple_of(start, 32), half), :]
        u, at = place_of[m]
        target = (
            own[u].at[at, pl.ds(0, half)],
            own[u].at[at, pl.ds(half, half)],
            hold[u].at[0, at],
            ahead[u].at[1, at],
            ahead[u].at[0, at],
            behind[u].at[0, at],
            behind[u].at[1, at],
            hold[u].at[1, at],
        )[k]
        return pltpu.make_async_copy(source, target, save_sem.at[m, k])

    for m, (left, second) in enumerate(((gate_t, 0), (up_t, 0), (hidden_t, 1))):

        def grad_chunk(j, carry, m=m, left=left, second=second):
            cols = pl.ds(pl.multiple_of(j * D_TILE, D_TILE), D_TILE)
            right = recv_ref[:, second, :, cols].reshape(n_rows, D_TILE)
            grads[m, :, cols] = contract(left[...], right, ((1,), (0,))).astype(jnp.bfloat16)
            return carry

        lax.fori_loop(0, width // D_TILE, grad_chunk, 0)
        for k in SEND_ORDER:
            save(m, k).start()

    def back_chunk(j, carry):
        cols = pl.ds(pl.multiple_of(j * D_TILE, D_TILE), D_TILE)
        out = contract(hidden[...], down_w[:, cols], ((1,), (0,)))
        back_ref[:, 0, :, cols] = out.astype(jnp.bfloat16).reshape(owners, cap, D_TILE)
        dx = contract(grad_pre[0], gate_w[cols], ((1,), (1,)))
        dx = dx + contract(grad_pre[1], up_w[cols], ((1,), (1,)))
        back_ref[:, 1, :, cols] = dx.astype(jnp.bfloat16).reshape(owners, cap, D_TILE)
        return carry

    lax.fori_loop(0, width // D_TILE, back_chunk, 0)
    for m in range(3):
        for k in SEND_ORDER:
            save(m, k).wait()


def expert(slot, units_of, here, recv, gate_weight, up_weight, down_weight, deps):
    owners, _, cap, width = recv.shape
    units = gate_weight.shape[2]
    rows = owners * cap
    half = units // 8
    anywhere = pl.BlockSpec(memory_space=pl.ANY)
    given = pl.BlockSpec((owners, 2, cap, width), lambda i: (0, 0, 0, 0))
    back = pl.BlockSpec((owners, 2, cap, width), lambda i: (0, 0, 0, 0))
    count = len(units_of)
    shapes = [(2, len(group), half, width) for group in units_of] * 3
    shapes += [(len(group), 2 * half, width) for group in units_of] + [(owners, 2, cap, width)]
    out = pl.pallas_call(
        functools.partial(expert_kernel, slot, units_of, len(deps)),
        grid=(1,),
        in_specs=[pl.BlockSpec(memory_space=pltpu.SMEM), given] + [anywhere] * (3 + len(deps)),
        out_specs=[anywhere] * (4 * count) + [back],
        out_shape=[jax.ShapeDtypeStruct(shape, jnp.bfloat16) for shape in shapes],
        scratch_shapes=[
            pltpu.VMEM((width, units), jnp.bfloat16),
            pltpu.VMEM((width, units), jnp.bfloat16),
            pltpu.VMEM((units, width), jnp.bfloat16),
            pltpu.VMEM((rows, units), jnp.bfloat16),
            pltpu.VMEM((2, rows, units), jnp.bfloat16),
            pltpu.VMEM((units, rows), jnp.bfloat16),
            pltpu.VMEM((units, rows), jnp.bfloat16),
            pltpu.VMEM((units, rows), jnp.bfloat16),
            pltpu.VMEM((3, units, width), jnp.bfloat16),
            pltpu.SemaphoreType.DMA((3, units // F_TILE)),
            pltpu.SemaphoreType.DMA((3, 8)),
        ],
        compiler_params=pltpu.CompilerParams(vmem_limit_bytes=VMEM),
        cost_estimate=pl.CostEstimate(
            flops=40 * rows * width * units,
            bytes_accessed=12 * width * units + 8 * rows * width,
            transcendentals=rows * units,
        ),
        name="expert",
    )(here, recv, gate_weight, up_weight, down_weight, *deps)
    return tuple(out[i * count : (i + 1) * count] for i in range(4)) + (out[4 * count],)


def combine_kernel(routes_ref, probs_ref, ids0_ref, ids1_ref, back0_ref, back1_ref, output_ref, grad_ref):
    width = output_ref.shape[1]
    output, grad = None, None
    for ids_ref, back_ref in ((ids0_ref, back0_ref), (ids1_ref, back1_ref)):
        rows = ids_ref.shape[0] * CAP
        chosen = slot_matrix(routes_ref[...], ids_ref[...])
        probs = slot_probs(routes_ref[...], probs_ref[...], ids_ref[...], chosen)
        high = probs.astype(jnp.bfloat16)
        low = (probs - high.astype(jnp.float32)).astype(jnp.bfloat16)
        out_rows = back_ref[:, 0].reshape(rows, width)
        dx_rows = back_ref[:, 1].reshape(rows, width)
        one_out = contract(high, out_rows, ((0,), (0,))) + contract(low, out_rows, ((0,), (0,)))
        one_grad = contract(chosen.astype(jnp.bfloat16), dx_rows, ((0,), (0,)))
        output = one_out if output is None else output + one_out
        grad = one_grad if grad is None else grad + one_grad
    output_ref[...] = output.astype(jnp.bfloat16)
    grad_ref[...] = grad.astype(jnp.bfloat16)


def combine(routes_t, probs_t, ids, backs, tok, width):
    row = jax.ShapeDtypeStruct((tok, width), jnp.bfloat16)
    return pl.pallas_call(
        combine_kernel,
        out_shape=[row, row],
        compiler_params=pltpu.CompilerParams(vmem_limit_bytes=VMEM),
        name="combine",
    )(routes_t, probs_t, *ids, *backs)


def shift(value, axis, by):
    n = lax.axis_size(axis)
    return lax.ppermute(value, axis, [(i, (i + by) % n) for i in range(n)])


def add(*terms):
    total = terms[0].astype(jnp.float32)
    for term in terms[1:]:
        total = total + term.astype(jnp.float32)
    return total.astype(jnp.bfloat16)


def spread_call(kernel, name, count, inputs, out_shapes, deps):
    specs = []
    for array, at in inputs:
        rows, width = array.shape[-2:]
        if at is None:
            specs.append(pl.BlockSpec((1, rows, width), lambda i: (i, 0, 0)))
        else:
            specs.append(pl.BlockSpec((1, 1, rows, width), functools.partial(lambda at, i: (at, i, 0, 0), at)))
    size = sum(shape[0] * shape[1] for shape in out_shapes)
    return pl.pallas_call(
        kernel,
        grid=(count,),
        in_specs=specs + [pl.BlockSpec(memory_space=pl.ANY)] * len(deps),
        out_specs=[pl.BlockSpec((1, *shape), lambda i: (i, 0, 0)) for shape in out_shapes],
        out_shape=[jax.ShapeDtypeStruct((count, *shape), jnp.bfloat16) for shape in out_shapes],
        compiler_params=pltpu.CompilerParams(vmem_limit_bytes=VMEM),
        cost_estimate=pl.CostEstimate(flops=2 * count * size, bytes_accessed=6 * count * size, transcendentals=0),
        name=name,
    )(*(array for array, _ in inputs), *deps)


def pair_kernel(hold_a_ref, hold_b_ref, far_a_ref, far_b_ref, *rest):
    pair_a_ref, pair_b_ref = rest[-2:]
    pair_a_ref[0] = add(hold_a_ref[0, 0], far_a_ref[0, 0])
    pair_b_ref[0] = add(hold_b_ref[0, 0], far_b_ref[0, 0])


def pair(hold, from_behind, from_ahead, deps):
    _, count, half, width = hold.shape
    inputs = [(hold, 0), (hold, 1), (from_behind, 0), (from_ahead, 0)]
    return spread_call(pair_kernel, "pair", count, inputs, [(half, width)] * 2, deps)


def finish_kernel(own_ref, near_a_ref, near_b_ref, pair_a_ref, pair_b_ref, *rest):
    sum_ref = rest[-1]
    half = pair_a_ref.shape[1]
    sum_ref[0, :half] = add(own_ref[0, :half], near_a_ref[0, 0], pair_a_ref[0])
    sum_ref[0, half:] = add(own_ref[0, half:], near_b_ref[0, 0], pair_b_ref[0])


def finish(own, from_behind, from_ahead, pair_a, pair_b, first, count, deps):
    _, quarter, width = own.shape
    half = quarter // 2

    def near(i):
        return (1, first + i, 0, 0)

    def at(i):
        return (first + i, 0, 0)

    return pl.pallas_call(
        finish_kernel,
        grid=(count,),
        in_specs=[
            pl.BlockSpec((1, quarter, width), at),
            pl.BlockSpec((1, 1, half, width), near),
            pl.BlockSpec((1, 1, half, width), near),
            pl.BlockSpec((1, half, width), at),
            pl.BlockSpec((1, half, width), at),
        ]
        + [pl.BlockSpec(memory_space=pl.ANY)] * len(deps),
        out_specs=pl.BlockSpec((1, quarter, width), lambda i: (i, 0, 0)),
        out_shape=jax.ShapeDtypeStruct((count, quarter, width), jnp.bfloat16),
        compiler_params=pltpu.CompilerParams(vmem_limit_bytes=VMEM),
        cost_estimate=pl.CostEstimate(
            flops=3 * count * quarter * width, bytes_accessed=8 * count * quarter * width, transcendentals=0
        ),
        name="finish",
    )(own, from_ahead, from_behind, pair_a, pair_b, *deps)


def place_kernel(stays_ref, own0_ref, other0_ref, own1_ref, other1_ref, *rest):
    out_ref = rest[-1]
    stays = stays_ref[0] == 1
    out_ref[:, 0, 0, :] = jnp.where(stays, own0_ref[0], other0_ref[0])
    out_ref[:, 0, 1, :] = jnp.where(stays, own1_ref[0], other1_ref[0])


def place(m, stays, parts, so_far, deps):
    _, quarter, width = parts[0][0].shape
    specs = [pl.BlockSpec((1, quarter, width), functools.partial(lambda at, i: (at, 0, 0), at)) for _, at in parts]
    given = ([] if so_far is None else [so_far]) + list(deps)
    return pl.pallas_call(
        place_kernel,
        grid=(1,),
        in_specs=[pl.BlockSpec(memory_space=pltpu.SMEM)] + specs + [pl.BlockSpec(memory_space=pl.ANY)] * len(given),
        out_specs=pl.BlockSpec((quarter, 1, 2, width), lambda i: (0, m, 0, 0)),
        out_shape=jax.ShapeDtypeStruct((quarter, 3, 2, width), jnp.bfloat16),
        input_output_aliases={} if so_far is None else {5: 0},
        compiler_params=pltpu.CompilerParams(vmem_limit_bytes=VMEM),
        cost_estimate=pl.CostEstimate(flops=2 * quarter * width, bytes_accessed=12 * quarter * width, transcendentals=0),
        name="place",
    )(stays, *(array for array, _ in parts), *given)


GROUPS = (((0, 1, 2),), ((0,), (1,), (2,)))


def local(tokens, cotangent, router_probs, routes, partner, gate_weight, up_weight, down_weight):
    tok, width = tokens.shape
    owners = lax.axis_size("expert")
    slots = gate_weight.shape[0]
    routes_t, probs_t = routes.T, router_probs.T
    ids = (partner[None, :] * slots + jnp.arange(slots, dtype=jnp.int32)[:, None]).reshape(slots, owners, 1)
    here = lax.axis_index("expert")
    plane = lax.axis_index("dp").reshape(1)
    stays = (jnp.sum(jnp.where(jnp.arange(owners) == here, partner, 0)) == here).astype(jnp.int32).reshape(1)
    sends = dispatch(routes_t, probs_t, ids, tokens, cotangent, (plane, stays))
    backs, final, after_pair = [], {}, ()
    for slot in range(slots):
        groups = GROUPS[slot]
        recv = lax.all_to_all(sends[slot], "expert", split_axis=0, concat_axis=0, tiled=True)
        ahead, behind, hold, own, back = expert(
            slot, groups, plane, recv, gate_weight, up_weight, down_weight, after_pair
        )
        backs.append(lax.all_to_all(back, "expert", split_axis=0, concat_axis=0, tiled=True))
        totals = [] if slot == 0 else totals
        for u, group in enumerate(groups):
            piece_ahead, piece_behind = ahead[u], behind[u]
            if slot == 1 and u > 0:
                piece_ahead, piece_behind, _ = lax.optimization_barrier((piece_ahead, piece_behind, totals[u - 1]))
            from_behind, from_ahead = shift(piece_ahead, "dp", 1), shift(piece_behind, "dp", -1)
            pair_a, pair_b = pair(hold[u], from_behind, from_ahead, ())
            if u == 0:
                after_pair = (pair_a, pair_b)
            pair_a, pair_b = shift(pair_a, "dp", 1), shift(pair_b, "dp", -1)
            at_once = len(group) if slot == 0 else 1
            for first in range(0, len(group), at_once):
                total = finish(own[u], from_behind, from_ahead, pair_a, pair_b, first, at_once, ())
                totals.append(total)
                other = shift(total, "expert", owners // 2)
                for at in range(at_once):
                    final[slot, group[first + at]] = [(total, at), (other, at)]
    output, token_grad = combine(routes_t, probs_t, (ids[0], ids[1]), backs, tok, width)
    grads = None
    for m in range(3):
        deps = (output,) if m == 2 else ()
        grads = place(m, stays, final[0, m] + final[1, m], grads, deps)
    return (output, token_grad, grads.transpose(0, 2, 1, 3))


def solution(mesh):
    rows = P(("expert", "dp"), None)
    by_slot = P("expert", None, None)
    return jax.shard_map(
        local,
        mesh=mesh,
        in_specs=(rows, rows, rows, rows, P(), by_slot, by_slot, by_slot),
        out_specs=(rows, rows, P("dp", "expert", None, None)),
        check_vma=False,
    )
```
